128 devices in a mesh: wide: 32 (over z, y, core), narrow: 4 (over x).
Axes of the slice: x: 4, y: 4, z: 4, core: 2. Of those that a mesh axis runs over, the one named last changes fastest.
Arguments:
- face_blocks: float32 [5120, 320, 320], P(('wide', 'narrow')), may hold values from -0.3125 to 0.3125
- face_elems: int32 [5120, 2], P(('wide', 'narrow')), may hold values from 0 to 1023, as said below
- coarse_slot: int32 [1024], replicated, may hold values from 0 to 1023, as said below
- prolong: float32 [320, 135], replicated, may hold values from -0.3125 to 0.3125
- fine_residual: float32 [1024, 320], P(('wide', 'narrow')), may hold values from -6 to 6
- block_inverse: float32 [1024, 135, 135], P(('wide', 'narrow'))
Outputs:
- fine_correction: float32 [1024, 320], P(('wide', 'narrow'))
- owned_blocks: float32 [12288, 135, 135], P(('wide', 'narrow'))
The draws below stay inside these ranges and needn't reach their ends.
Inputs may be any that keep to these rules, and one draw needn't show every extreme that they name: `coarse_slot`: A permutation: every element has its own coarse row. `face_elems`: the row and column elements of a face differ. With the owner of an element being coarse_slot // 32, among the 40 faces of each device (aligned blocks of 40 rows, devices in the order wide then narrow) at most 3 have row elements of any one owner, and for each narrow index one owner takes exactly 3 faces from every device with that narrow index.
All inputs are finite; a program needn't handle non-finite values.
Results may differ from the reference program's by a relative error of at most 0.000075.
Values sent between devices are 32-bit elements; how exact they have to be, the bound alone decides.
A program may use at most 192 MiB of HBM per device.

```python
import jax
import jax.numpy as jnp
from jax import lax

NF = 320
NC = 135
FACE_DEV = 40
EL_DEV = 8
CAP = 3
FACES = 5120
ELEMS = 1024
EL_OWN = 32
N_WIDE = 32
N_NARROW = 4


def face_pattern(key):
    keys = jax.random.split(jax.random.fold_in(key, 7), 6)
    slot_table = jax.random.permutation(keys[0], ELEMS).astype(jnp.int32)
    inverse = jnp.argsort(slot_table).astype(jnp.int32)
    block_count = N_WIDE * N_NARROW
    narrow_of = jnp.arange(block_count, dtype=jnp.int32) % N_NARROW
    hottest = jax.random.randint(keys[1], (N_NARROW,), 0, N_WIDE, dtype=jnp.int32)[narrow_of]
    spread_len = (N_WIDE - 1) * CAP
    spread_idx = jnp.arange(spread_len, dtype=jnp.int32)
    candidate = (hottest[:, None] + 1 + spread_idx[None, :] // CAP) % N_WIDE
    scores = jax.random.randint(keys[2], (block_count, spread_len), 0, 65536, dtype=jnp.int32) * spread_len + spread_idx[None, :]
    shuffled = jnp.take_along_axis(candidate, jnp.argsort(scores, axis=1), axis=1)[:, :FACE_DEV - CAP]
    owners = jnp.concatenate([jnp.broadcast_to(hottest[:, None], (block_count, CAP)), shuffled], axis=1)
    face_idx = jnp.arange(FACE_DEV, dtype=jnp.int32)
    scores_two = jax.random.randint(keys[3], (block_count, FACE_DEV), 0, 65536, dtype=jnp.int32) * FACE_DEV + face_idx[None, :]
    owners = jnp.take_along_axis(owners, jnp.argsort(scores_two, axis=1), axis=1).reshape(-1)
    row_slot = owners * EL_OWN + jax.random.randint(keys[4], (FACES,), 0, EL_OWN, dtype=jnp.int32)
    col_slot = (row_slot + jax.random.randint(keys[5], (FACES,), 1, ELEMS, dtype=jnp.int32)) % ELEMS
    pairs = jnp.stack([inverse[row_slot], inverse[col_slot]], axis=1).astype(jnp.int32)
    return (slot_table, pairs)


def draw_face_elems(key, part):
    return face_pattern(key)[1]


def draw_coarse_slot(key, part):
    return face_pattern(key)[0]


def draw_block_inverse(key, part):
    keys = jax.random.split(jax.random.fold_in(key, 11), 2)
    identity = (jnp.arange(NC)[:, None] == jnp.arange(NC)[None, :]).astype(jnp.float32)
    noise = jax.random.normal(keys[0], (ELEMS, NC, NC), jnp.float32) * (0.5 * NC ** (-0.5))
    diagonal = 1.0 + jax.random.uniform(keys[1], (ELEMS, 1, 1), jnp.float32, -0.2, 0.2)
    return (diagonal * identity + noise).astype(jnp.float32)


def level_of(rng, extent, shards, low, largest):
    gain, own = 1.0, jax.random.fold_in(rng, 6)
    for axis_at, shards_of in shards:
        draws = jnp.exp(jax.random.uniform(jax.random.fold_in(own, axis_at), (shards_of,), jnp.float32, low / len(shards), largest / len(shards)))
        gain = gain * jnp.repeat(draws, extent[axis_at] // shards_of).reshape([-1 if axis == axis_at else 1 for axis in range(len(extent))])
    return gain


def scatter_about(stream_key, dims, scale, most, cuts=(), kind=jnp.bfloat16):
    loudness = level_of(stream_key, dims, cuts, -0.22, 0.18) if cuts else 1.0
    drawn = jax.random.normal(stream_key, dims, jnp.float32) * scale * loudness
    return jnp.minimum(jnp.maximum(drawn, -most), most).astype(kind)


def setup_inputs(seed: int = 0) -> dict:
    arg_keys = jax.random.split(jax.random.key(seed), 7)
    face_blocks = scatter_about(arg_keys[0], (FACES, NF, NF), (0.6 * (NC * FACE_DEV // EL_DEV) ** -0.5), 0.3125, ((0, 128),), jnp.float32)
    face_elems = draw_face_elems(jax.random.fold_in(arg_keys[6], 71), 0)
    coarse_slot = draw_coarse_slot(jax.random.fold_in(arg_keys[6], 71), 0)
    prolong = scatter_about(arg_keys[3], (NF, NC), NF ** -0.5, 0.3125, (), jnp.float32)
    fine_residual = scatter_about(arg_keys[4], (ELEMS, NF), 1.0, 6.0, ((0, 128),), jnp.float32)
    block_inverse = draw_block_inverse(jax.random.fold_in(arg_keys[6], 71), 0)
    return dict(face_blocks=face_blocks, face_elems=face_elems, coarse_slot=coarse_slot, prolong=prolong, fine_residual=fine_residual, block_inverse=block_inverse)


DAMPING = 0.7
PRECISE = lax.Precision.HIGHEST


def face_terms(inputs, prolong):
    blocks, vectors = inputs
    applied = jnp.einsum("fij,jc->fic", blocks, prolong, precision=PRECISE)
    coarse_blocks = jnp.einsum("ia,fic->fac", prolong, applied, precision=PRECISE)
    products = jnp.einsum("fac,fc->fa", coarse_blocks, vectors, precision=PRECISE)
    return coarse_blocks, products


def partial_terms(prolong):
    def apply_group(inputs):
        return face_terms(inputs, prolong)
    return apply_group


def reference(face_blocks, face_elems, coarse_slot, prolong, fine_residual, block_inverse):
    device_count = N_WIDE * N_NARROW
    coarse_rhs = jnp.dot(fine_residual, prolong, precision=PRECISE)
    sweep_one = DAMPING * jnp.einsum("snm,sm->sn", block_inverse, coarse_rhs, precision=PRECISE)
    slot_pairs = jnp.take(coarse_slot, face_elems, axis=0)
    row_slot = slot_pairs[:, 0]
    col_slot = slot_pairs[:, 1]
    column_values = jnp.take(sweep_one, col_slot, axis=0)
    grouped_blocks = face_blocks.reshape(device_count, FACE_DEV, NF, NF)
    grouped_values = column_values.reshape(device_count, FACE_DEV, NC)
    blocks_all, contributions = lax.map(partial_terms(prolong), (grouped_blocks, grouped_values))
    coupling = jax.ops.segment_sum(contributions.reshape(-1, NC), row_slot, num_segments=ELEMS)
    update = (1.0 - DAMPING) * coarse_rhs - coupling
    sweep_two = sweep_one + DAMPING * jnp.einsum("snm,sm->sn", block_inverse, update, precision=PRECISE)
    correction = jnp.dot(sweep_two, prolong.T, precision=PRECISE)

    owner_of = (row_slot // EL_OWN).astype(jnp.int32).reshape(device_count, FACE_DEV)
    selector = (owner_of[:, :, None] == jnp.arange(N_WIDE, dtype=jnp.int32)[None, None, :]).astype(jnp.int32)
    ranking = jnp.sum(selector * (jnp.cumsum(selector, axis=1) - 1), axis=2)
    device = jnp.arange(device_count, dtype=jnp.int32)[:, None]
    wide_of = device // N_NARROW
    narrow_of = device % N_NARROW
    placing = (((owner_of * N_NARROW + narrow_of) * N_WIDE + wide_of) * CAP + ranking).astype(jnp.int32)
    owned = jnp.zeros((device_count * N_WIDE * CAP, NC, NC), jnp.float32)
    owned = owned.at[placing.reshape(-1)].set(blocks_all.reshape(-1, NC, NC))
    return correction, owned
```

```python
import functools

import jax
import jax.numpy as jnp
from jax import lax
from jax.experimental import pallas as pl
from jax.experimental.pallas import tpu as pltpu
from jax.sharding import PartitionSpec as P

DAMPING = 0.7
PRECISE = lax.Precision.HIGHEST
MESH = pl.DeviceIdType.MESH

NF = 320
NC = 135
ROWS = 136
FACES = 40
WIDE = 32
NARROW = 4
CAP = 3
SLOTS = WIDE * CAP
OWN = 32
STEP = 13


def tables_kernel(faces, slots, face_o, valid_o, col_o, row_o, count):
    def clear(i, _):
        face_o[i] = 0
        valid_o[i] = 0
        col_o[i] = 0
        row_o[i] = -1
        return 0

    def clear_count(i, _):
        count[i] = 0
        return 0

    lax.fori_loop(0, SLOTS, clear, 0)
    lax.fori_loop(0, WIDE, clear_count, 0)

    def place(f, _):
        row = slots[faces[0, f]]
        owner = row // OWN
        rank = count[owner]
        count[owner] = rank + 1
        at = owner * CAP + rank
        face_o[at] = f
        valid_o[at] = 1
        col_o[at] = slots[faces[1, f]]
        row_o[at] = row % OWN
        return 0

    lax.fori_loop(0, FACES, place, 0)


def slot_tables(face_elems, coarse_slot):
    smem = pl.BlockSpec(memory_space=pltpu.SMEM)
    return pl.pallas_call(
        tables_kernel,
        out_shape=[jax.ShapeDtypeStruct((SLOTS,), jnp.int32)] * 4,
        in_specs=[smem] * 2,
        out_specs=[smem] * 4,
        scratch_shapes=[pltpu.SMEM((WIDE,), jnp.int32)],
        name="tables",
    )(face_elems.T, coarse_slot)


def split(x):
    high = x.astype(jnp.bfloat16)
    return high, (x - high.astype(jnp.float32)).astype(jnp.bfloat16)


def dot(a, b):
    return jnp.dot(a, b, preferred_element_type=jnp.float32)


def dot_t(a, b):
    return lax.dot_general(
        a, b, (((1,), (1,)), ((), ())), precision=PRECISE, preferred_element_type=jnp.float32
    )


def jacobi(inverse, vectors):
    row = lax.broadcasted_iota(jnp.int32, (8, NC), 0)
    out = jnp.zeros((8, NC), jnp.float32)
    for s in range(8):
        out = jnp.where(row == s, dot_t(vectors, inverse[:, s, :]), out)
    return out


def exchange_kernel(
    face_t, valid_t, col_t, row_t, faces_hbm, pt, values, inverse, rhs, one,
    fine_o, main_o, rem_o,
    faces, wide_pt, p_hi, p_lo, pt_hi, pt_lo, main_s, rem_s, sums, y_s, y_r, x_s, x_r,
    face_sem, main_ss, main_rs, rem_ss, rem_rs, y_ss, y_rs, x_ss, x_rs, own_sem,
):
    w = lax.axis_index("wide")
    n = lax.axis_index("narrow")

    def load(i):
        part = pl.ds(i * 8, 8)
        return pltpu.make_async_copy(faces_hbm.at[part], faces.at[part], face_sem.at[i])

    for i in range(5):
        load(i).start()

    def partner(offset, sign):
        z, y, c = w // 8, (w // 2) % 4, w % 2
        dz, dy, dc = offset // 8, (offset // 2) % 4, offset % 2
        return ((z + sign * dz + 4) % 4) * 8 + ((y + sign * dy + 4) % 4) * 2 + (c + dc) % 2

    barrier = pltpu.get_barrier_semaphore()

    def greet(i, _):
        pl.semaphore_signal(barrier, inc=1, device_id=(partner(i, 1), n), device_id_type=MESH)
        return 0

    lax.fori_loop(1, WIDE, greet, 0)
    for i in range(1, NARROW):
        pl.semaphore_signal(barrier, inc=1, device_id=(w, (n + i) % NARROW), device_id_type=MESH)

    wide_pt[...] = jnp.zeros_like(wide_pt)
    wide_pt[0:NC, :] = pt[...]
    pt_hi[...], pt_lo[...] = split(wide_pt[0:144, :])
    p_hi[...], p_lo[...] = split(wide_pt[...].T)

    lane = lax.broadcasted_iota(jnp.int32, (ROWS, 128), 1)
    sub = lax.broadcasted_iota(jnp.int32, (ROWS, 1), 0)
    sums[...] = jnp.where(lax.broadcasted_iota(jnp.int32, (ROWS, 128), 0) == NC, -1.0, 0.0)

    def main_copy(offset, to, home):
        return pltpu.make_async_remote_copy(
            src_ref=main_s.at[pl.ds(to * CAP, CAP)],
            dst_ref=main_o.at[pl.ds(home * CAP, CAP)],
            send_sem=main_ss.at[offset], recv_sem=main_rs.at[offset],
            device_id=(to, n), device_id_type=MESH,
        )

    def rem_copy(offset, to, home):
        return pltpu.make_async_remote_copy(
            src_ref=rem_s.at[pl.ds(to * CAP, CAP)],
            dst_ref=rem_o.at[pl.ds(home * CAP, CAP)],
            send_sem=rem_ss.at[offset], recv_sem=rem_rs.at[offset],
            device_id=(to, n), device_id_type=MESH,
        )

    def y_copy(offset, to, home):
        return pltpu.make_async_remote_copy(
            src_ref=y_s.at[to], dst_ref=y_r.at[home],
            send_sem=y_ss.at[offset], recv_sem=y_rs.at[offset],
            device_id=(to, n), device_id_type=MESH,
        )

    def compute(to):
        def slot(k, _):
            s = to * CAP + k
            block = faces[face_t[s]]
            high, low = split(block)
            applied = dot(high, p_hi[...]) + dot(low, p_hi[...]) + dot(high, p_lo[...])
            high, low = split(applied)
            both = dot(pt_hi[...], high) + dot(pt_lo[...], high) + dot(pt_hi[...], low)
            both = jnp.where(valid_t[s] > 0, both[0:ROWS, :], 0.0)
            main_s[s] = both[:, 0:128]
            corner = pltpu.roll(both[128:ROWS, 128:256], 0, 1, stride=8, stride_axis=0)
            main_s[s, NC:ROWS, :] = jnp.sum(corner, axis=0, keepdims=True)
            rem_s[s] = both[0:128, 128:256].T[0:8, :]
            v = values[pl.ds(col_t[s], 1), :]
            y = jnp.sum(both[:, 0:NC] * v, axis=1, keepdims=True)
            y = jnp.where(sub == NC, row_t[s].astype(jnp.float32), y)
            sums[...] = jnp.where(lane == to * 4 + k, y, sums[...])
            return 0

        lax.fori_loop(0, CAP, slot, 0)

    for i in range(5):
        load(i).wait()
    pl.semaphore_wait(barrier, WIDE + NARROW - 2)

    def send(step, _):
        offset = ((step + 1) * STEP) % WIDE
        to = partner(offset, 1)
        compute(to)
        main_copy(offset, to, w).start()
        rem_copy(offset, to, w).start()
        return 0

    lax.fori_loop(0, WIDE - 1, send, 0)
    compute(w)
    mine = pl.ds(w * CAP, CAP)
    own_main = pltpu.make_async_copy(main_s.at[mine], main_o.at[mine], own_sem.at[0])
    own_rem = pltpu.make_async_copy(rem_s.at[mine], rem_o.at[mine], own_sem.at[1])
    own_main.start()
    own_rem.start()

    by_slot = jnp.concatenate([sums[0:128, :].T, jnp.pad(sums[128:ROWS, :].T, ((0, 0), (0, 120)))], axis=0)
    for to in range(WIDE):
        y_s[to, 0:3, :] = by_slot[4 * to : 4 * to + 3, :]
        y_s[to, 3:6, :] = by_slot[128 + 4 * to : 128 + 4 * to + 3, :]
        y_s[to, 6:8, :] = jnp.zeros((2, 128), jnp.float32)

    def send_y(offset, _):
        y_copy(offset, partner(offset, 1), w).start()
        return 0

    lax.fori_loop(1, WIDE, send_y, 0)
    y_r[w] = y_s[w]

    def wait_y(offset, _):
        y_copy(offset, partner(offset, 1), partner(offset, -1)).wait_recv()
        return 0

    lax.fori_loop(1, WIDE, wait_y, 0)

    terms = y_r[...].reshape(WIDE * 8, 128)
    labels = terms.T[7:8, :]
    place = lax.broadcasted_iota(jnp.int32, (OWN, WIDE * 8), 1) % 8
    of_row = lax.broadcasted_iota(jnp.int32, (OWN, WIDE * 8), 0).astype(jnp.float32)
    tail = jnp.where((labels == of_row) & (place >= 3) & (place < 6), 1.0, 0.0)
    head = pltpu.roll(tail, WIDE * 8 - 3, 1)
    head_sum = jnp.dot(head, terms, precision=PRECISE, preferred_element_type=jnp.float32)
    tail_sum = jnp.dot(tail, terms, precision=PRECISE, preferred_element_type=jnp.float32)
    for i in range(NARROW):
        x_s[i, 0:8, :] = head_sum[8 * i : 8 * i + 8, :]
        x_s[i, 8:16, :] = tail_sum[8 * i : 8 * i + 8, :]

    def x_copy(i, home):
        to = (n + i) % NARROW
        return pltpu.make_async_remote_copy(
            src_ref=x_s.at[to], dst_ref=x_r.at[home],
            send_sem=x_ss.at[i], recv_sem=x_rs.at[i],
            device_id=(w, to), device_id_type=MESH,
        )

    for i in range(1, NARROW):
        x_copy(i, n).start()
    x_r[n] = x_s[n]
    for i in range(1, NARROW):
        x_copy(i, (n + NARROW - i) % NARROW).wait_recv()
    total = x_r[0] + x_r[1] + x_r[2] + x_r[3]
    coupling = jnp.concatenate([total[0:8, :], total[8:16, :]], axis=1)[:, 0:NC]
    update = (1.0 - DAMPING) * rhs[...] - coupling
    two = one[...] + DAMPING * jacobi(inverse, update)
    fine_o[...] = jnp.dot(two, pt[...], precision=PRECISE, preferred_element_type=jnp.float32)

    def finish(offset, _):
        to, source = partner(offset, 1), partner(offset, -1)
        for copy in (main_copy, rem_copy):
            copy(offset, to, source).wait_recv()
        for copy in (main_copy, rem_copy, y_copy):
            copy(offset, to, w).wait_send()
        return 0

    lax.fori_loop(1, WIDE, finish, 0)
    for i in range(1, NARROW):
        x_copy(i, n).wait_send()
    own_main.wait()
    own_rem.wait()


def exchange(tables, face_blocks, pt, values, inverse, rhs, one):
    smem = pl.BlockSpec(memory_space=pltpu.SMEM)
    vmem = pl.BlockSpec(memory_space=pltpu.VMEM)
    anywhere = pl.BlockSpec(memory_space=pl.ANY)
    f32, bf16, dma = jnp.float32, jnp.bfloat16, pltpu.SemaphoreType.DMA
    return pl.pallas_call(
        exchange_kernel,
        out_shape=[
            jax.ShapeDtypeStruct((8, NF), f32),
            jax.ShapeDtypeStruct((SLOTS, ROWS, 128), f32),
            jax.ShapeDtypeStruct((SLOTS, 8, 128), f32),
        ],
        in_specs=[smem] * 4 + [anywhere] + [vmem] * 5,
        out_specs=[vmem, anywhere, anywhere],
        scratch_shapes=[
            pltpu.VMEM((FACES, NF, NF), f32),
            pltpu.VMEM((256, NF), f32),
            pltpu.VMEM((NF, 256), bf16),
            pltpu.VMEM((NF, 256), bf16),
            pltpu.VMEM((144, NF), bf16),
            pltpu.VMEM((144, NF), bf16),
            pltpu.VMEM((SLOTS, ROWS, 128), f32),
            pltpu.VMEM((SLOTS, 8, 128), f32),
            pltpu.VMEM((ROWS, 128), f32),
            pltpu.VMEM((WIDE, 8, 128), f32),
            pltpu.VMEM((WIDE, 8, 128), f32),
            pltpu.VMEM((NARROW, 16, 128), f32),
            pltpu.VMEM((NARROW, 16, 128), f32),
            dma((5,)),
        ]
        + [dma((WIDE,))] * 6
        + [dma((NARROW,))] * 2
        + [dma((2,))],
        compiler_params=pltpu.CompilerParams(
            collective_id=0, has_side_effects=True, vmem_limit_bytes=48 << 20
        ),
        cost_estimate=pl.CostEstimate(flops=10**10, bytes_accessed=35 * 10**6, transcendentals=0),
        name="exchange",
    )(*tables, face_blocks, pt, values, inverse, rhs, one)


def unpack_kernel(main, rem, out, edge):
    i = pl.program_id(0)

    @pl.when(i == 0)
    def _():
        for c in range(NC - 128):
            edge[c] = rem[:, c, :].T

    for r in range(8):
        out[r, 0:128, :] = main[:, r, :].T

    @pl.when(i < 16)
    def _():
        for c in range(NC - 128):
            out[:, 128 + c, :] = edge[c, pl.ds(pl.multiple_of(i * 8, 8), 8), :]

    @pl.when(i == 16)
    def _():
        corner = main[:, 7, :].T
        for r in range(NC - 128):
            out[r, 128:NC, :] = corner[8 * r : 8 * r + NC - 128, :]


def unpack(main, rem):
    return pl.pallas_call(
        unpack_kernel,
        grid=(17,),
        out_shape=jax.ShapeDtypeStruct((NC, NC, SLOTS), jnp.float32),
        in_specs=[
            pl.BlockSpec((SLOTS, 8, 128), lambda i: (0, i, 0)),
            pl.BlockSpec((SLOTS, 8, 128), lambda i: (0, 0, 0)),
        ],
        out_specs=pl.BlockSpec((8, NC, SLOTS), lambda i: (i, 0, 0)),
        scratch_shapes=[pltpu.VMEM((NC - 128, 128, SLOTS), jnp.float32)],
        compiler_params=pltpu.CompilerParams(vmem_limit_bytes=32 << 20),
        name="unpack",
    )(main, rem)


def local(face_blocks, face_elems, coarse_slot, prolong, fine_residual, block_inverse):
    rhs = jnp.dot(fine_residual, prolong, precision=PRECISE)
    one = DAMPING * jnp.einsum("snm,sm->sn", block_inverse, rhs, precision=PRECISE)
    values = lax.all_gather(one, ("wide", "narrow"), axis=0, tiled=True)
    tables = slot_tables(face_elems, coarse_slot)
    fine, main, rem = exchange(
        tables, face_blocks, prolong.T, values, jnp.transpose(block_inverse, (1, 0, 2)), rhs, one
    )
    return fine, jnp.transpose(unpack(main, rem), (2, 0, 1))


def solution(mesh):
    placed = (
        P(("wide", "narrow"), None, None),
        P(("wide", "narrow"), None),
        P(),
        P(),
        P(("wide", "narrow"), None),
        P(("wide", "narrow"), None, None),
    )
    return jax.shard_map(
        local,
        mesh=mesh,
        in_specs=placed,
        out_specs=(P(("wide", "narrow"), None), P(("wide", "narrow"), None, None)),
        check_vma=False,
    )
```

```python
import functools

import jax
import jax.numpy as jnp
from jax import lax
from jax.experimental import pallas as pl
from jax.experimental.pallas import tpu as pltpu
from jax.sharding import PartitionSpec as P

DAMPING = 0.7
PRECISE = lax.Precision.HIGHEST
MESH = pl.DeviceIdType.MESH

NF = 320
NC = 135
ROWS = 136
FACES = 40
WIDE = 32
NARROW = 4
CAP = 3
SLOTS = WIDE * CAP
OWN = 32
PAIRS = (
    (1, 1), (3, 3), (1, 3), (3, 1), (2, 1), (0, 3), (2, 3), (0, 1),
    (1, 2), (3, 0), (3, 2), (1, 0), (2, 0), (0, 2), (2, 2),
)
CODES = tuple(
    sum((4 * dz + dy) * 16**i for i, (dz, dy) in enumerate(PAIRS[at : at + 7])) for at in (0, 7, 14)
)
GATHER_AT, SPREAD_AT = 2, 9


def offset_at(step):
    i = step + 3
    pair = i // 4 * 2 + i % 2 - 2
    core = i // 2 % 2
    last = step // 29
    pair = pair * (1 - last) + 14 * last
    core = core * (1 - last) + (step - 29) * last
    part = pair // 7
    first, second, third = (part - 1) * (part - 2) // 2, part * (2 - part), part * (part - 1) // 2
    code = CODES[0] * first + CODES[1] * second + CODES[2] * third
    offset = lax.shift_right_logical(code, 4 * (pair % 7)) % 16 * 2 + core
    start, end = 1 - (step + 30) // 31 + step // 31, step // 31
    return (offset * (1 - start) + start) * (1 - end)


def tables_kernel(faces, slots, face_o, valid_o, col_o, row_o, count):
    def clear(i, _):
        face_o[i] = 0
        valid_o[i] = 0
        col_o[i] = 0
        row_o[i] = -1
        return 0

    def clear_count(i, _):
        count[i] = 0
        return 0

    lax.fori_loop(0, SLOTS, clear, 0)
    lax.fori_loop(0, WIDE, clear_count, 0)

    def place(f, _):
        row = slots[faces[0, f]]
        owner = row // OWN
        rank = count[owner]
        count[owner] = rank + 1
        at = owner * CAP + rank
        face_o[at] = f
        valid_o[at] = 1
        col_o[at] = slots[faces[1, f]]
        row_o[at] = row % OWN
        return 0

    lax.fori_loop(0, FACES, place, 0)


def slot_tables(face_elems, coarse_slot):
    smem = pl.BlockSpec(memory_space=pltpu.SMEM)
    return pl.pallas_call(
        tables_kernel,
        out_shape=[jax.ShapeDtypeStruct((SLOTS,), jnp.int32)] * 4,
        in_specs=[smem] * 2,
        out_specs=[smem] * 4,
        scratch_shapes=[pltpu.SMEM((WIDE,), jnp.int32)],
        name="tables",
    )(face_elems.T, coarse_slot)


def split(x):
    high = x.astype(jnp.bfloat16)
    return high, (x - high.astype(jnp.float32)).astype(jnp.bfloat16)


def dot(a, b):
    return jnp.dot(a, b, preferred_element_type=jnp.float32)


def dot_t(a, b):
    return lax.dot_general(
        a, b, (((1,), (1,)), ((), ())), precision=PRECISE, preferred_element_type=jnp.float32
    )


def jacobi(inverse, vectors):
    row = lax.broadcasted_iota(jnp.int32, (8, NC), 0)
    out = jnp.zeros((8, NC), jnp.float32)
    for s in range(8):
        out = jnp.where(row == s, dot_t(vectors, inverse[:, s, :]), out)
    return out


def exchange_kernel(
    face_t, valid_t, col_t, row_t, faces_hbm, pt, residual, inverse,
    fine_o, main_o, rem_o,
    faces, wide_pt, p_hi, p_lo, pt_hi, pt_lo, main_s, rem_s, edge_s, sums, y_s, y_r, x_s, x_r,
    v_s, v_r, values,
    face_sem, main_ss, main_rs, rem_ss, rem_rs, y_ss, y_rs, g_ss, g_rs, x_ss, x_rs, v_ss, v_rs,
    core_sem, own_sem,
):
    w = lax.axis_index("wide")
    n = lax.axis_index("narrow")

    def load(i):
        part = pl.ds(i * 8, 8)
        return pltpu.make_async_copy(faces_hbm.at[part], faces.at[part], face_sem.at[i])

    for i in range(5):
        load(i).start()

    def partner(offset, sign):
        z, y, c = w // 8, (w // 2) % 4, w % 2
        dz, dy, dc = offset // 8, (offset // 2) % 4, offset % 2
        return ((z + sign * dz + 4) % 4) * 8 + ((y + sign * dy + 4) % 4) * 2 + (c + dc) % 2

    barrier = pltpu.get_barrier_semaphore()

    def greet(i, _):
        pl.semaphore_signal(barrier, inc=1, device_id=(partner(i, 1), n), device_id_type=MESH)
        return 0

    lax.fori_loop(1, WIDE, greet, 0)
    for i in range(1, NARROW):
        pl.semaphore_signal(barrier, inc=1, device_id=(w, (n + i) % NARROW), device_id_type=MESH)

    wide_pt[...] = jnp.zeros_like(wide_pt)
    wide_pt[0:NC, :] = pt[...]
    pt_hi[...], pt_lo[...] = split(wide_pt[0:144, :])
    p_hi[...], p_lo[...] = split(wide_pt[...].T)

    rhs = dot_t(residual[...], pt[...])
    one = DAMPING * jacobi(inverse, rhs)
    zq, core = w // 2, w % 2
    record = core * 16 + zq
    v_s[0] = one[:, 0:128]
    v_s[1] = pltpu.roll(jnp.pad(one[:, 128:NC], ((0, 0), (0, 256 - NC))), 8 * n, 1)

    def v_copy(i, home):
        return pltpu.make_async_remote_copy(
            src_ref=v_s, dst_ref=v_r.at[home], send_sem=v_ss.at[i], recv_sem=v_rs.at[i],
            device_id=(w, (n + i) % NARROW), device_id_type=MESH,
        )

    def g_copy(q, home):
        chip = (zq // 4 + q // 4) % 4 * 4 + (zq % 4 + q % 4) % 4
        return pltpu.make_async_remote_copy(
            src_ref=values.at[record], dst_ref=values.at[core * 16 + home],
            send_sem=g_ss.at[q], recv_sem=g_rs.at[q],
            device_id=(chip * 2 + core, n), device_id_type=MESH,
        )

    def core_copy(half):
        part = pl.ds(half * 16, 16)
        return pltpu.make_async_remote_copy(
            src_ref=values.at[part], dst_ref=values.at[part],
            send_sem=core_sem.at[0], recv_sem=core_sem.at[1],
            device_id=(zq * 2 + 1 - core, n), device_id_type=MESH,
        )

    lane = lax.broadcasted_iota(jnp.int32, (ROWS, 128), 1)
    sub = lax.broadcasted_iota(jnp.int32, (ROWS, 1), 0)
    sums[...] = jnp.where(lax.broadcasted_iota(jnp.int32, (ROWS, 128), 0) == NC, -1.0, 0.0)

    def main_copy(offset, to, home):
        return pltpu.make_async_remote_copy(
            src_ref=main_s.at[pl.ds(to * CAP, CAP)],
            dst_ref=main_o.at[pl.ds(home * CAP, CAP)],
            send_sem=main_ss.at[offset], recv_sem=main_rs.at[offset],
            device_id=(to, n), device_id_type=MESH,
        )

    def rem_copy(offset, to, home):
        return pltpu.make_async_remote_copy(
            src_ref=rem_s.at[pl.ds(to * CAP, CAP)],
            dst_ref=rem_o.at[pl.ds(home * CAP, CAP)],
            send_sem=rem_ss.at[offset], recv_sem=rem_rs.at[offset],
            device_id=(to, n), device_id_type=MESH,
        )

    def y_copy(offset, to, home):
        return pltpu.make_async_remote_copy(
            src_ref=y_s.at[to], dst_ref=y_r.at[home],
            send_sem=y_ss.at[offset], recv_sem=y_rs.at[offset],
            device_id=(to, n), device_id_type=MESH,
        )

    def compute(to):
        applied = []
        for k in range(CAP):
            high, low = split(faces[face_t[to * CAP + k]])
            applied.append(dot(high, p_hi[...]) + dot(low, p_hi[...]) + dot(high, p_lo[...]))
        for k in range(CAP):
            s = to * CAP + k
            high, low = split(applied[k])
            both = dot(pt_hi[...], high) + dot(pt_lo[...], high) + dot(pt_hi[...], low)
            both = jnp.where(valid_t[s] > 0, both[0:ROWS, :], 0.0)
            edge = both[:, 128:256]
            main_s[s] = both[:, 0:128]
            corner = pltpu.roll(edge[128:ROWS, :], 0, 1, stride=8, stride_axis=0)
            main_s[s, NC:ROWS, :] = jnp.sum(corner, axis=0, keepdims=True)
            rem_s[s] = edge[0:128, :].T[0:8, :]
            edge_s[s] = edge

    pl.semaphore_wait(barrier, WIDE + NARROW - 2)
    for i in range(1, NARROW):
        v_copy(i, n).start()
    v_r[n] = v_s[...]
    for i in range(5):
        load(i).wait()

    def send(step, _):
        offset = offset_at(step)
        to = partner(offset, 1)
        compute(to)

        @pl.when(step < WIDE - 1)
        def _():
            main_copy(offset, to, w).start()
            rem_copy(offset, to, w).start()

        @pl.when(step == GATHER_AT)
        def _():
            for i in range(1, NARROW):
                v_copy(i, (n + NARROW - i) % NARROW).wait_recv()
            for i in range(NARROW):
                values[record, i] = v_r[i, 0]
            values[record, NARROW] = v_r[0, 1] + v_r[1, 1] + v_r[2, 1] + v_r[3, 1]

            def spread(q, _):
                g_copy(q, zq).start()
                return 0

            lax.fori_loop(1, 16, spread, 0)

        @pl.when(step == SPREAD_AT)
        def _():
            def arrive(q, _):
                home = (zq // 4 - q // 4 + 4) % 4 * 4 + (zq % 4 - q % 4 + 4) % 4
                g_copy(q, home).wait_recv()
                return 0

            lax.fori_loop(1, 16, arrive, 0)
            core_copy(core).start()

        return 0

    lax.fori_loop(0, WIDE, send, 0)
    mine = pl.ds(w * CAP, CAP)
    own_main = pltpu.make_async_copy(main_s.at[mine], main_o.at[mine], own_sem.at[0])
    own_rem = pltpu.make_async_copy(rem_s.at[mine], rem_o.at[mine], own_sem.at[1])
    own_main.start()
    own_rem.start()
    core_copy(1 - core).wait_recv()

    def apply(to, _):
        for k in range(CAP):
            s = to * CAP + k
            device = col_t[s] // 8
            row = pl.ds(col_t[s] % 8, 1)
            held = device // NARROW
            at = held % 2 * 16 + held // 2
            head = values[at, device % NARROW, row, :]
            tail = pltpu.roll(values[at, NARROW, row, :], (128 - 8 * (device % NARROW)) % 128, 1)
            y = jnp.sum(main_s[s] * head + edge_s[s] * tail, axis=1, keepdims=True)
            y = jnp.where(sub == NC, row_t[s].astype(jnp.float32), y)
            sums[...] = jnp.where(lane == to * 4 + k, y, sums[...])
        return 0

    lax.fori_loop(0, WIDE, apply, 0)

    by_slot = jnp.concatenate([sums[0:128, :].T, jnp.pad(sums[128:ROWS, :].T, ((0, 0), (0, 120)))], axis=0)
    for to in range(WIDE):
        y_s[to, 0:3, :] = by_slot[4 * to : 4 * to + 3, :]
        y_s[to, 3:6, :] = by_slot[128 + 4 * to : 128 + 4 * to + 3, :]
        y_s[to, 6:8, :] = jnp.zeros((2, 128), jnp.float32)

    def send_y(offset, _):
        y_copy(offset, partner(offset, 1), w).start()
        return 0

    lax.fori_loop(1, WIDE, send_y, 0)
    y_r[w] = y_s[w]

    def wait_y(offset, _):
        y_copy(offset, partner(offset, 1), partner(offset, -1)).wait_recv()
        return 0

    lax.fori_loop(1, WIDE, wait_y, 0)

    terms = y_r[...].reshape(WIDE * 8, 128)
    labels = terms.T[7:8, :]
    place = lax.broadcasted_iota(jnp.int32, (OWN, WIDE * 8), 1) % 8
    of_row = lax.broadcasted_iota(jnp.int32, (OWN, WIDE * 8), 0).astype(jnp.float32)
    tail = jnp.where((labels == of_row) & (place >= 3) & (place < 6), 1.0, 0.0)
    head = pltpu.roll(tail, WIDE * 8 - 3, 1)
    head_sum = jnp.dot(head, terms, precision=PRECISE, preferred_element_type=jnp.float32)
    tail_sum = jnp.dot(tail, terms, precision=PRECISE, preferred_element_type=jnp.float32)
    for i in range(NARROW):
        x_s[i, 0:8, :] = head_sum[8 * i : 8 * i + 8, :]
        x_s[i, 8:16, :] = tail_sum[8 * i : 8 * i + 8, :]

    def x_copy(i, home):
        to = (n + i) % NARROW
        return pltpu.make_async_remote_copy(
            src_ref=x_s.at[to], dst_ref=x_r.at[home],
            send_sem=x_ss.at[i], recv_sem=x_rs.at[i],
            device_id=(w, to), device_id_type=MESH,
        )

    for i in range(1, NARROW):
        x_copy(i, n).start()
    x_r[n] = x_s[n]
    for i in range(1, NARROW):
        x_copy(i, (n + NARROW - i) % NARROW).wait_recv()
    total = x_r[0] + x_r[1] + x_r[2] + x_r[3]
    coupling = jnp.concatenate([total[0:8, :], total[8:16, :]], axis=1)[:, 0:NC]
    update = (1.0 - DAMPING) * rhs - coupling
    two = one + DAMPING * jacobi(inverse, update)
    fine_o[...] = jnp.dot(two, pt[...], precision=PRECISE, preferred_element_type=jnp.float32)

    def finish(offset, _):
        to, source = partner(offset, 1), partner(offset, -1)
        for copy in (main_copy, rem_copy):
            copy(offset, to, source).wait_recv()
        for copy in (main_copy, rem_copy, y_copy):
            copy(offset, to, w).wait_send()
        return 0

    lax.fori_loop(1, WIDE, finish, 0)

    def finish_spread(q, _):
        g_copy(q, zq).wait_send()
        return 0

    lax.fori_loop(1, 16, finish_spread, 0)
    core_copy(core).wait_send()
    for i in range(1, NARROW):
        x_copy(i, n).wait_send()
        v_copy(i, n).wait_send()
    own_main.wait()
    own_rem.wait()


def exchange(tables, face_blocks, pt, residual, inverse):
    smem = pl.BlockSpec(memory_space=pltpu.SMEM)
    vmem = pl.BlockSpec(memory_space=pltpu.VMEM)
    anywhere = pl.BlockSpec(memory_space=pl.ANY)
    f32, bf16, dma = jnp.float32, jnp.bfloat16, pltpu.SemaphoreType.DMA
    return pl.pallas_call(
        exchange_kernel,
        out_shape=[
            jax.ShapeDtypeStruct((8, NF), f32),
            jax.ShapeDtypeStruct((SLOTS, ROWS, 128), f32),
            jax.ShapeDtypeStruct((SLOTS, 8, 128), f32),
        ],
        in_specs=[smem] * 4 + [anywhere] + [vmem] * 3,
        out_specs=[vmem, anywhere, anywhere],
        scratch_shapes=[
            pltpu.VMEM((FACES, NF, NF), f32),
            pltpu.VMEM((256, NF), f32),
            pltpu.VMEM((NF, 256), bf16),
            pltpu.VMEM((NF, 256), bf16),
            pltpu.VMEM((144, NF), bf16),
            pltpu.VMEM((144, NF), bf16),
            pltpu.VMEM((SLOTS, ROWS, 128), f32),
            pltpu.VMEM((SLOTS, 8, 128), f32),
            pltpu.VMEM((SLOTS, ROWS, 128), f32),
            pltpu.VMEM((ROWS, 128), f32),
            pltpu.VMEM((WIDE, 8, 128), f32),
            pltpu.VMEM((WIDE, 8, 128), f32),
            pltpu.VMEM((NARROW, 16, 128), f32),
            pltpu.VMEM((NARROW, 16, 128), f32),
            pltpu.VMEM((2, 8, 128), f32),
            pltpu.VMEM((NARROW, 2, 8, 128), f32),
            pltpu.VMEM((WIDE, NARROW + 1, 8, 128), f32),
            dma((5,)),
        ]
        + [dma((WIDE,))] * 6
        + [dma((16,))] * 2
        + [dma((NARROW,))] * 4
        + [dma((2,))] * 2,
        compiler_params=pltpu.CompilerParams(
            collective_id=0, has_side_effects=True, vmem_limit_bytes=52 << 20
        ),
        cost_estimate=pl.CostEstimate(flops=10**10, bytes_accessed=35 * 10**6, transcendentals=0),
        name="exchange",
    )(*tables, face_blocks, pt, residual, inverse)


def unpack_kernel(main, rem, out, edge):
    i = pl.program_id(0)

    @pl.when(i == 0)
    def _():
        for c in range(NC - 128):
            edge[c] = rem[:, c, :].T

    for r in range(8):
        out[r, 0:128, :] = main[:, r, :].T

    @pl.when(i < 16)
    def _():
        for c in range(NC - 128):
            out[:, 128 + c, :] = edge[c, pl.ds(pl.multiple_of(i * 8, 8), 8), :]

    @pl.when(i == 16)
    def _():
        corner = main[:, 7, :].T
        for r in range(NC - 128):
            out[r, 128:NC, :] = corner[8 * r : 8 * r + NC - 128, :]


def unpack(main, rem):
    return pl.pallas_call(
        unpack_kernel,
        grid=(17,),
        out_shape=jax.ShapeDtypeStruct((NC, NC, SLOTS), jnp.float32),
        in_specs=[
            pl.BlockSpec((SLOTS, 8, 128), lambda i: (0, i, 0)),
            pl.BlockSpec((SLOTS, 8, 128), lambda i: (0, 0, 0)),
        ],
        out_specs=pl.BlockSpec((8, NC, SLOTS), lambda i: (i, 0, 0)),
        scratch_shapes=[pltpu.VMEM((NC - 128, 128, SLOTS), jnp.float32)],
        compiler_params=pltpu.CompilerParams(vmem_limit_bytes=32 << 20),
        name="unpack",
    )(main, rem)


def local(face_blocks, face_elems, coarse_slot, prolong, fine_residual, block_inverse):
    tables = slot_tables(face_elems, coarse_slot)
    fine, main, rem = exchange(
        tables, face_blocks, prolong.T, fine_residual, jnp.transpose(block_inverse, (1, 0, 2))
    )
    return fine, jnp.transpose(unpack(main, rem), (2, 0, 1))


def solution(mesh):
    placed = (
        P(("wide", "narrow"), None, None),
        P(("wide", "narrow"), None),
        P(),
        P(),
        P(("wide", "narrow"), None),
        P(("wide", "narrow"), None, None),
    )
    return jax.shard_map(
        local,
        mesh=mesh,
        in_specs=placed,
        out_specs=(P(("wide", "narrow"), None), P(("wide", "narrow"), None, None)),
        check_vma=False,
    )
```

```python
import functools

import jax
import jax.numpy as jnp
from jax import lax
from jax.experimental import pallas as pl
from jax.experimental.pallas import tpu as pltpu
from jax.sharding import PartitionSpec as P

DAMPING = 0.7
PRECISE = lax.Precision.HIGHEST
MESH = pl.DeviceIdType.MESH

NF = 320
NC = 135
ROWS = 136
PART = 45
FACES = 40
WIDE = 32
NARROW = 4
CAP = 3
SLOTS = WIDE * CAP
OWN = 32
PAIRS = (
    (1, 1), (3, 3), (1, 3), (3, 1), (2, 1), (0, 3), (2, 3), (0, 1),
    (1, 2), (3, 0), (3, 2), (1, 0), (2, 0), (0, 2), (2, 2),
)
CODES = tuple(
    sum((4 * dz + dy) * 16**i for i, (dz, dy) in enumerate(PAIRS[at : at + 7])) for at in (0, 7, 14)
)
GATHER_AT, SPREAD_AT = 2, 9
HELD = 26


def offset_at(step):
    last, near = step // 28, step // 30
    pair = (step // 4 * 2 + step % 2) * (1 - last) + 14 * last
    core = step // 2 % 2 * (1 - last) + (step - 28) * last
    part = pair // 7
    first, second, third = (part - 1) * (part - 2) // 2, part * (2 - part), part * (part - 1) // 2
    code = CODES[0] * first + CODES[1] * second + CODES[2] * third
    offset = lax.shift_right_logical(code, 4 * (pair % 7)) % 16 * 2 + core
    return offset * (1 - near) + (31 - step) * near


def tables_kernel(faces, slots, word_o, count):
    def clear(i, _):
        word_o[i] = 0
        return 0

    def clear_count(i, _):
        count[i] = 0
        return 0

    lax.fori_loop(0, 128, clear, 0, unroll=8)
    lax.fori_loop(0, WIDE, clear_count, 0, unroll=8)

    def place(f, _):
        row = slots[faces[0, f]]
        owner = lax.shift_right_logical(row, 5)
        rank = count[owner]
        count[owner] = rank + 1
        word_o[owner * CAP + rank] = (1 << 21) + (row & (OWN - 1)) * 65536 + slots[faces[1, f]] * 64 + f
        return 0

    lax.fori_loop(0, FACES, place, 0, unroll=4)


def slot_table(face_elems, coarse_slot):
    smem = pl.BlockSpec(memory_space=pltpu.SMEM)
    return pl.pallas_call(
        tables_kernel,
        out_shape=jax.ShapeDtypeStruct((128,), jnp.int32),
        in_specs=[smem] * 2,
        out_specs=smem,
        scratch_shapes=[pltpu.SMEM((WIDE,), jnp.int32)],
        name="tables",
    )(face_elems.T, coarse_slot)


def shifted(word, by, bits):
    return lax.shift_right_logical(word, by) & ((1 << bits) - 1)


def split(x):
    high = x.astype(jnp.bfloat16)
    return high, (x - high.astype(jnp.float32)).astype(jnp.bfloat16)


def dot(a, b):
    return jnp.dot(a, b, preferred_element_type=jnp.float32)


def dot_t(a, b):
    return lax.dot_general(
        a, b, (((1,), (1,)), ((), ())), precision=PRECISE, preferred_element_type=jnp.float32
    )


def jacobi(inverse, vectors):
    row = lax.broadcasted_iota(jnp.int32, (8, NC), 0)
    out = jnp.zeros((8, NC), jnp.float32)
    for s in range(8):
        out = jnp.where(row == s, dot_t(vectors, inverse[:, s, :]), out)
    return out


def exchange_kernel(
    word_hbm, faces_hbm, pt_hbm, residual_hbm, inverse_hbm,
    fine_o, main_o, rem_o,
    word, pt, residual, inverse, faces, wide_pt, p_hi, p_lo, pt_hi, pt_lo, main_s, rem_s, edge_s, sums, y_s, y_r, x_s, x_r,
    v_s, v_r, values,
    in_sem, face_sem, main_ss, main_rs, rem_ss, rem_rs, y_ss, y_rs, g_ss, g_rs, x_ss, x_rs, v_ss, v_rs,
    core_sem, own_sem,
):
    w = lax.axis_index("wide")
    n = lax.axis_index("narrow")

    def load(i):
        part = pl.ds(i * 8, 8)
        return pltpu.make_async_copy(faces_hbm.at[part], faces.at[part], face_sem.at[i])

    inputs = [
        pltpu.make_async_copy(source, target, in_sem.at[i])
        for i, (source, target) in enumerate(
            ((pt_hbm, pt), (residual_hbm, residual), (inverse_hbm, inverse), (word_hbm, word))
        )
    ]
    for copy in inputs:
        copy.start()
    for i in range(5):
        load(i).start()

    def partner(offset, sign):
        z, y, c = w // 8, (w // 2) % 4, w % 2
        dz, dy, dc = offset // 8, (offset // 2) % 4, offset % 2
        return ((z + sign * dz + 4) % 4) * 8 + ((y + sign * dy + 4) % 4) * 2 + (c + dc) % 2

    barrier = pltpu.get_barrier_semaphore()

    def greet(i, _):
        pl.semaphore_signal(barrier, inc=1, device_id=(partner(i, 1), n), device_id_type=MESH)
        return 0

    lax.fori_loop(1, WIDE, greet, 0)
    for i in range(1, NARROW):
        pl.semaphore_signal(barrier, inc=1, device_id=(w, (n + i) % NARROW), device_id_type=MESH)

    for copy in inputs:
        copy.wait()
    wide_pt[...] = jnp.zeros_like(wide_pt)
    wide_pt[0:NC, :] = pt[...]
    pt_hi[...], pt_lo[...] = split(wide_pt[0:144, :])
    p_hi[...], p_lo[...] = split(wide_pt[...].T)

    rhs = dot_t(residual[...], pt[...])
    one = DAMPING * jacobi(inverse, rhs)
    zq, core = w // 2, w % 2
    record = core * 16 + zq
    v_s[0] = one[:, 0:128]
    v_s[1] = pltpu.roll(jnp.pad(one[:, 128:NC], ((0, 0), (0, 256 - NC))), 8 * n, 1)

    def v_copy(i, home):
        return pltpu.make_async_remote_copy(
            src_ref=v_s, dst_ref=v_r.at[home], send_sem=v_ss.at[i], recv_sem=v_rs.at[i],
            device_id=(w, (n + i) % NARROW), device_id_type=MESH,
        )

    def g_copy(q, home):
        chip = (zq // 4 + q // 4) % 4 * 4 + (zq % 4 + q % 4) % 4
        return pltpu.make_async_remote_copy(
            src_ref=values.at[record], dst_ref=values.at[core * 16 + home],
            send_sem=g_ss.at[q], recv_sem=g_rs.at[q],
            device_id=(chip * 2 + core, n), device_id_type=MESH,
        )

    def core_copy(half):
        part = pl.ds(half * 16, 16)
        return pltpu.make_async_remote_copy(
            src_ref=values.at[part], dst_ref=values.at[part],
            send_sem=core_sem.at[0], recv_sem=core_sem.at[1],
            device_id=(zq * 2 + 1 - core, n), device_id_type=MESH,
        )

    lane = lax.broadcasted_iota(jnp.int32, (ROWS, 128), 1)
    sub = lax.broadcasted_iota(jnp.int32, (ROWS, 1), 0)
    sums[...] = jnp.where(lax.broadcasted_iota(jnp.int32, (ROWS, 128), 0) == NC, -1.0, 0.0)

    def main_copy(offset, to, home):
        return pltpu.make_async_remote_copy(
            src_ref=main_s.at[pl.ds(to * CAP, CAP)],
            dst_ref=main_o.at[pl.ds(home * CAP, CAP)],
            send_sem=main_ss.at[offset], recv_sem=main_rs.at[offset],
            device_id=(to, n), device_id_type=MESH,
        )

    def rem_copy(offset, to, home):
        return pltpu.make_async_remote_copy(
            src_ref=rem_s.at[pl.ds(to * CAP, CAP)],
            dst_ref=rem_o.at[pl.ds(home * CAP, CAP)],
            send_sem=rem_ss.at[offset], recv_sem=rem_rs.at[offset],
            device_id=(to, n), device_id_type=MESH,
        )

    def y_copy(offset, to, home):
        return pltpu.make_async_remote_copy(
            src_ref=y_s.at[to], dst_ref=y_r.at[home],
            send_sem=y_ss.at[offset], recv_sem=y_rs.at[offset],
            device_id=(to, n), device_id_type=MESH,
        )

    def compute(to):
        applied = []
        for k in range(CAP):
            high, low = split(faces[shifted(word[to * CAP + k], 0, 6)])
            applied.append(dot(high, p_hi[...]) + dot(low, p_hi[...]) + dot(high, p_lo[...]))
        for k in range(CAP):
            s = to * CAP + k
            high, low = split(applied[k])
            both = dot(pt_hi[...], high) + dot(pt_lo[...], high) + dot(pt_hi[...], low)
            both = jnp.where(shifted(word[s], 21, 1) > 0, both[0:ROWS, :], 0.0)
            edge = both[:, 128:256]
            main_s[s] = both[:, 0:128]
            corner = pltpu.roll(edge[128:ROWS, :], 0, 1, stride=8, stride_axis=0)
            main_s[s, NC:ROWS, :] = jnp.sum(corner, axis=0, keepdims=True)
            rem_s[s] = edge[0:128, :].T[0:8, :]
            edge_s[s] = edge

    pl.semaphore_wait(barrier, WIDE + NARROW - 2)
    for i in range(1, NARROW):
        v_copy(i, n).start()
    v_r[n] = v_s[...]
    for i in range(5):
        load(i).wait()

    def send(step, _):
        offset = offset_at(step)
        to = partner(offset, 1)
        compute(to)

        @pl.when((step < HELD) | (step == WIDE - 2))
        def _():
            main_copy(offset, to, w).start()
            rem_copy(offset, to, w).start()

        @pl.when(step == GATHER_AT)
        def _():
            for i in range(1, NARROW):
                v_copy(i, (n + NARROW - i) % NARROW).wait_recv()
            for i in range(NARROW):
                values[record, i] = v_r[i, 0]
            values[record, NARROW] = v_r[0, 1] + v_r[1, 1] + v_r[2, 1] + v_r[3, 1]

            def spread(q, _):
                g_copy(q, zq).start()
                return 0

            lax.fori_loop(1, 16, spread, 0)

        @pl.when(step == SPREAD_AT)
        def _():
            def arrive(q, _):
                home = (zq // 4 - q // 4 + 4) % 4 * 4 + (zq % 4 - q % 4 + 4) % 4
                g_copy(q, home).wait_recv()
                return 0

            lax.fori_loop(1, 16, arrive, 0)
            core_copy(core).start()

        return 0

    lax.fori_loop(0, WIDE, send, 0)
    mine = pl.ds(w * CAP, CAP)
    own_main = pltpu.make_async_copy(main_s.at[mine], main_o.at[mine], own_sem.at[0])
    own_rem = pltpu.make_async_copy(rem_s.at[mine], rem_o.at[mine], own_sem.at[1])
    own_main.start()
    own_rem.start()
    core_copy(1 - core).wait_recv()

    def apply(to, _):
        for k in range(CAP):
            s = to * CAP + k
            row = pl.ds(shifted(word[s], 6, 3), 1)
            narrow = shifted(word[s], 9, 2)
            at = shifted(word[s], 11, 1) * 16 + shifted(word[s], 12, 4)
            head = values[at, narrow, row, :]
            tail = pltpu.roll(values[at, NARROW, row, :], (128 - 8 * narrow) % 128, 1)
            y = jnp.sum(main_s[s] * head + edge_s[s] * tail, axis=1, keepdims=True)
            label = shifted(word[s], 16, 5) * shifted(word[s], 21, 1) - 1 + shifted(word[s], 21, 1)
            y = jnp.where(sub == NC, label.astype(jnp.float32), y)
            sums[...] = jnp.where(lane == to * 4 + k, y, sums[...])
        return 0

    lax.fori_loop(0, WIDE, apply, 0)

    by_slot = jnp.concatenate([sums[0:128, :].T, jnp.pad(sums[128:ROWS, :].T, ((0, 0), (0, 120)))], axis=0)
    for to in range(WIDE):
        y_s[to, 0:3, :] = by_slot[4 * to : 4 * to + 3, :]
        y_s[to, 3:6, :] = by_slot[128 + 4 * to : 128 + 4 * to + 3, :]
        y_s[to, 6:8, :] = jnp.zeros((2, 128), jnp.float32)

    def send_y(offset, _):
        y_copy(offset, partner(offset, 1), w).start()
        return 0

    lax.fori_loop(1, WIDE, send_y, 0)
    y_r[w] = y_s[w]

    def send_held(step, _):
        offset = offset_at(step)
        to = partner(offset, 1)
        main_copy(offset, to, w).start()
        rem_copy(offset, to, w).start()
        return 0

    lax.fori_loop(HELD, WIDE - 2, send_held, 0)

    def wait_y(offset, _):
        y_copy(offset, partner(offset, 1), partner(offset, -1)).wait_recv()
        return 0

    lax.fori_loop(1, WIDE, wait_y, 0)

    terms = y_r[...].reshape(WIDE * 8, 128)
    labels = terms.T[7:8, :]
    place = lax.broadcasted_iota(jnp.int32, (OWN, WIDE * 8), 1) % 8
    of_row = lax.broadcasted_iota(jnp.int32, (OWN, WIDE * 8), 0).astype(jnp.float32)
    tail = jnp.where((labels == of_row) & (place >= 3) & (place < 6), 1.0, 0.0)
    head = pltpu.roll(tail, WIDE * 8 - 3, 1)
    head_sum = jnp.dot(head, terms, precision=PRECISE, preferred_element_type=jnp.float32)
    tail_sum = jnp.dot(tail, terms, precision=PRECISE, preferred_element_type=jnp.float32)
    for i in range(NARROW):
        x_s[i, 0:8, :] = head_sum[8 * i : 8 * i + 8, :]
        x_s[i, 8:16, :] = tail_sum[8 * i : 8 * i + 8, :]

    def x_copy(i, home):
        to = (n + i) % NARROW
        return pltpu.make_async_remote_copy(
            src_ref=x_s.at[to], dst_ref=x_r.at[home],
            send_sem=x_ss.at[i], recv_sem=x_rs.at[i],
            device_id=(w, to), device_id_type=MESH,
        )

    for i in range(1, NARROW):
        x_copy(i, n).start()
    x_r[n] = x_s[n]
    for i in range(1, NARROW):
        x_copy(i, (n + NARROW - i) % NARROW).wait_recv()
    total = x_r[0] + x_r[1] + x_r[2] + x_r[3]
    coupling = jnp.concatenate([total[0:8, :], total[8:16, :]], axis=1)[:, 0:NC]
    update = (1.0 - DAMPING) * rhs - coupling
    two = one + DAMPING * jacobi(inverse, update)
    fine_o[...] = jnp.dot(two, pt[...], precision=PRECISE, preferred_element_type=jnp.float32)

    def finish(offset, _):
        to, source = partner(offset, 1), partner(offset, -1)
        for copy in (main_copy, rem_copy):
            copy(offset, to, source).wait_recv()
        for copy in (main_copy, rem_copy, y_copy):
            copy(offset, to, w).wait_send()
        return 0

    lax.fori_loop(1, WIDE, finish, 0)

    def finish_spread(q, _):
        g_copy(q, zq).wait_send()
        return 0

    lax.fori_loop(1, 16, finish_spread, 0)
    core_copy(core).wait_send()
    for i in range(1, NARROW):
        x_copy(i, n).wait_send()
        v_copy(i, n).wait_send()
    own_main.wait()
    own_rem.wait()


def exchange(table, face_blocks, pt, residual, inverse):
    hbm = pl.BlockSpec(memory_space=pltpu.HBM)
    vmem = pl.BlockSpec(memory_space=pltpu.VMEM)
    anywhere = pl.BlockSpec(memory_space=pl.ANY)
    f32, bf16, dma = jnp.float32, jnp.bfloat16, pltpu.SemaphoreType.DMA
    return pl.pallas_call(
        exchange_kernel,
        out_shape=[
            jax.ShapeDtypeStruct((8, NF), f32),
            jax.ShapeDtypeStruct((SLOTS, ROWS, 128), f32),
            jax.ShapeDtypeStruct((SLOTS, 8, 128), f32),
        ],
        in_specs=[hbm] * 5,
        out_specs=[vmem, anywhere, anywhere],
        scratch_shapes=[
            pltpu.SMEM((128,), jnp.int32),
            pltpu.VMEM((NC, NF), f32),
            pltpu.VMEM((8, NF), f32),
            pltpu.VMEM((NC, 8, NC), f32),
            pltpu.VMEM((FACES, NF, NF), f32),
            pltpu.VMEM((256, NF), f32),
            pltpu.VMEM((NF, 256), bf16),
            pltpu.VMEM((NF, 256), bf16),
            pltpu.VMEM((144, NF), bf16),
            pltpu.VMEM((144, NF), bf16),
            pltpu.VMEM((SLOTS, ROWS, 128), f32),
            pltpu.VMEM((SLOTS, 8, 128), f32),
            pltpu.VMEM((SLOTS, ROWS, 128), f32),
            pltpu.VMEM((ROWS, 128), f32),
            pltpu.VMEM((WIDE, 8, 128), f32),
            pltpu.VMEM((WIDE, 8, 128), f32),
            pltpu.VMEM((NARROW, 16, 128), f32),
            pltpu.VMEM((NARROW, 16, 128), f32),
            pltpu.VMEM((2, 8, 128), f32),
            pltpu.VMEM((NARROW, 2, 8, 128), f32),
            pltpu.VMEM((WIDE, NARROW + 1, 8, 128), f32),
            dma((4,)),
            dma((5,)),
        ]
        + [dma((WIDE,))] * 6
        + [dma((16,))] * 2
        + [dma((NARROW,))] * 4
        + [dma((2,))] * 2,
        compiler_params=pltpu.CompilerParams(
            collective_id=0, has_side_effects=True, vmem_limit_bytes=42 << 20
        ),
        cost_estimate=pl.CostEstimate(flops=10**10, bytes_accessed=35 * 10**6, transcendentals=0),
        name="exchange",
    )(table, face_blocks, pt, residual, inverse)


def unpack_kernel(main, rem, fine_in, out, fine, edge):
    i = pl.program_id(0)
    rest = NC - 128

    def row(a):
        return main[pl.ds(a, SLOTS, stride=ROWS), :].T

    @pl.when(i == 0)
    def _():
        fine[...] = fine_in[...]
        for c in range(rest):
            edge[c] = rem[pl.ds(c, SLOTS, stride=8), :].T

    for j in range(NC // PART):

        @pl.when(i == j)
        def _(j=j):
            for r in range(PART):
                out[r, 0:128, :] = row(j * PART + r)
            size = min(PART, 128 - j * PART)
            for c in range(rest):
                out[0:size, 128 + c, :] = edge[c, j * PART : j * PART + size, :]
            if size < PART:
                corner = row(NC)
                for r in range(rest):
                    out[size + r, 128:NC, :] = corner[8 * r : 8 * r + rest, :]


def unpack(main, rem, fine):
    vmem = pl.BlockSpec(memory_space=pltpu.VMEM)
    return pl.pallas_call(
        unpack_kernel,
        grid=(NC // PART,),
        out_shape=[
            jax.ShapeDtypeStruct((NC, NC, SLOTS), jnp.float32),
            jax.ShapeDtypeStruct((8, NF), jnp.float32),
        ],
        in_specs=[vmem] * 3,
        out_specs=[
            pl.BlockSpec((PART, NC, SLOTS), lambda i: (i, 0, 0)),
            pl.BlockSpec((8, NF), lambda i: (0, 0)),
        ],
        scratch_shapes=[pltpu.VMEM((NC - 128, 128, SLOTS), jnp.float32)],
        compiler_params=pltpu.CompilerParams(vmem_limit_bytes=40 << 20),
        name="unpack",
    )(main, rem, fine)


def local(face_blocks, face_elems, coarse_slot, prolong, fine_residual, block_inverse):
    table = slot_table(face_elems, coarse_slot)
    fine, main, rem = exchange(
        table, face_blocks, prolong.T, fine_residual, jnp.transpose(block_inverse, (1, 0, 2))
    )
    owned, fine = unpack(main.reshape(SLOTS * ROWS, 128), rem.reshape(SLOTS * 8, 128), fine)
    return fine, jnp.transpose(owned, (2, 0, 1))


def solution(mesh):
    placed = (
        P(("wide", "narrow"), None, None),
        P(("wide", "narrow"), None),
        P(),
        P(),
        P(("wide", "narrow"), None),
        P(("wide", "narrow"), None, None),
    )
    return jax.shard_map(
        local,
        mesh=mesh,
        in_specs=placed,
        out_specs=(P(("wide", "narrow"), None), P(("wide", "narrow"), None, None)),
        check_vma=False,
    )
```

```python
import functools

import jax
import jax.numpy as jnp
from jax import lax
from jax.experimental import pallas as pl
from jax.experimental.pallas import tpu as pltpu
from jax.sharding import PartitionSpec as P

DAMPING = 0.7
PRECISE = lax.Precision.HIGHEST
MESH = pl.DeviceIdType.MESH

NF = 320
NC = 135
ROWS = 136
PART = 45
FACES = 40
WIDE = 32
NARROW = 4
CAP = 3
SLOTS = WIDE * CAP
OWN = 32
PAIRS = (
    (1, 1), (3, 3), (1, 3), (3, 1), (2, 1), (0, 3), (2, 3), (0, 1),
    (1, 2), (3, 0), (3, 2), (1, 0), (2, 0), (0, 2), (2, 2),
)
CODES = tuple(
    sum((4 * dz + dy) * 16**i for i, (dz, dy) in enumerate(PAIRS[at : at + 7])) for at in (0, 7, 14)
)
CORE_AT, NARROW_AT = 2, 5
HELD = 26


def offset_at(step):
    last, near = step // 28, step // 30
    pair = (step // 4 * 2 + step % 2) * (1 - last) + 14 * last
    core = step // 2 % 2 * (1 - last) + (step - 28) * last
    part = pair // 7
    first, second, third = (part - 1) * (part - 2) // 2, part * (2 - part), part * (part - 1) // 2
    code = CODES[0] * first + CODES[1] * second + CODES[2] * third
    offset = lax.shift_right_logical(code, 4 * (pair % 7)) % 16 * 2 + core
    return offset * (1 - near) + (31 - step) * near


def slot_words(faces, slots):
    lane = lax.broadcasted_iota(jnp.int32, (1, 128), 1)

    def place(f, words):
        first, second, third = words
        row = slots[faces[0, f]]
        word = (1 << 21) + (row & (OWN - 1)) * 65536 + slots[faces[1, f]] * 64 + f
        here = lane == lax.shift_right_logical(row, 5)
        third = jnp.where(here & (second > 0), word, third)
        second = jnp.where(here & (first > 0) & (second == 0), word, second)
        first = jnp.where(here & (first == 0), word, first)
        return first, second, third

    empty = jnp.zeros((1, 128), jnp.int32)
    return lax.fori_loop(0, FACES, place, (empty, empty, empty), unroll=4)


def shifted(word, by, bits):
    return lax.shift_right_logical(word, by) & ((1 << bits) - 1)


def split(x):
    high = x.astype(jnp.bfloat16)
    return high, (x - high.astype(jnp.float32)).astype(jnp.bfloat16)


def dot(a, b):
    return jnp.dot(a, b, preferred_element_type=jnp.float32)


def dot_t(a, b):
    return lax.dot_general(
        a, b, (((1,), (1,)), ((), ())), precision=PRECISE, preferred_element_type=jnp.float32
    )


def jacobi(inverse, vectors):
    row = lax.broadcasted_iota(jnp.int32, (8, NC), 0)
    out = jnp.zeros((8, NC), jnp.float32)
    for s in range(8):
        out = jnp.where(row == s, dot_t(vectors, inverse[:, s, :]), out)
    return out


def exchange_kernel(
    elems_hbm, slots_hbm, faces_hbm, pt_hbm, residual_hbm, inverse_hbm,
    fine_o, main_o, rem_o,
    elems, slots, words, word, pt, residual, inverse, faces, wide_pt, p_hi, p_lo, pt_hi, pt_lo, main_s, rem_s, edge_s, sums, y_s, y_r, x_s, x_r,
    values,
    in_sem, word_sem, face_sem, main_ss, main_rs, rem_ss, rem_rs, y_ss, y_rs, g_ss, g_rs, x_ss, x_rs, v_ss, v_rs,
    core_sem, own_sem,
):
    w = lax.axis_index("wide")
    n = lax.axis_index("narrow")

    def load(i):
        part = pl.ds(i * 8, 8)
        return pltpu.make_async_copy(faces_hbm.at[part], faces.at[part], face_sem.at[i])

    inputs = [
        pltpu.make_async_copy(source, target, in_sem.at[i])
        for i, (source, target) in enumerate(
            ((elems_hbm, elems), (slots_hbm, slots), (pt_hbm, pt), (residual_hbm, residual), (inverse_hbm, inverse))
        )
    ]
    for copy in inputs:
        copy.start()
    for i in range(5):
        load(i).start()

    def partner(offset, sign):
        z, y, c = w // 8, (w // 2) % 4, w % 2
        dz, dy, dc = offset // 8, (offset // 2) % 4, offset % 2
        return ((z + sign * dz + 4) % 4) * 8 + ((y + sign * dy + 4) % 4) * 2 + (c + dc) % 2

    barrier = pltpu.get_barrier_semaphore()

    def greet(i, _):
        pl.semaphore_signal(barrier, inc=1, device_id=(partner(i, 1), n), device_id_type=MESH)
        return 0

    lax.fori_loop(1, WIDE, greet, 0)
    for i in range(1, NARROW):
        pl.semaphore_signal(barrier, inc=1, device_id=(w, (n + i) % NARROW), device_id_type=MESH)

    for copy in inputs:
        copy.wait()
    wide_pt[...] = jnp.zeros_like(wide_pt)
    wide_pt[0:NC, :] = pt[...]
    pt_hi[...], pt_lo[...] = split(wide_pt[0:144, :])
    p_hi[...], p_lo[...] = split(wide_pt[...].T)

    rhs = dot_t(residual[...], pt[...])
    one = DAMPING * jacobi(inverse, rhs)
    zq, core = w // 2, w % 2
    values[n, core * 16 + zq, 0] = one[:, 0:128]
    values[n, core * 16 + zq, 1] = jnp.pad(one[:, 128:NC], ((0, 0), (0, 256 - NC)))

    def v_copy(i, home):
        return pltpu.make_async_remote_copy(
            src_ref=values.at[n], dst_ref=values.at[home], send_sem=v_ss.at[i], recv_sem=v_rs.at[i],
            device_id=(w, (n + i) % NARROW), device_id_type=MESH,
        )

    def g_copy(q, home):
        chip = (zq // 4 + q // 4) % 4 * 4 + (zq % 4 + q % 4) % 4
        return pltpu.make_async_remote_copy(
            src_ref=values.at[n, core * 16 + zq], dst_ref=values.at[n, core * 16 + home],
            send_sem=g_ss.at[q], recv_sem=g_rs.at[q],
            device_id=(chip * 2 + core, n), device_id_type=MESH,
        )

    def core_copy(half):
        part = pl.ds(half * 16, 16)
        return pltpu.make_async_remote_copy(
            src_ref=values.at[n, part], dst_ref=values.at[n, part],
            send_sem=core_sem.at[0], recv_sem=core_sem.at[1],
            device_id=(zq * 2 + 1 - core, n), device_id_type=MESH,
        )

    lane = lax.broadcasted_iota(jnp.int32, (ROWS, 128), 1)
    sub = lax.broadcasted_iota(jnp.int32, (ROWS, 1), 0)
    sums[...] = jnp.where(lax.broadcasted_iota(jnp.int32, (ROWS, 128), 0) == NC, -1.0, 0.0)

    def main_copy(offset, to, home):
        return pltpu.make_async_remote_copy(
            src_ref=main_s.at[pl.ds(to * CAP, CAP)],
            dst_ref=main_o.at[pl.ds(home * CAP, CAP)],
            send_sem=main_ss.at[offset], recv_sem=main_rs.at[offset],
            device_id=(to, n), device_id_type=MESH,
        )

    def rem_copy(offset, to, home):
        return pltpu.make_async_remote_copy(
            src_ref=rem_s.at[pl.ds(to * CAP, CAP)],
            dst_ref=rem_o.at[pl.ds(home * CAP, CAP)],
            send_sem=rem_ss.at[offset], recv_sem=rem_rs.at[offset],
            device_id=(to, n), device_id_type=MESH,
        )

    def y_copy(offset, to, home):
        return pltpu.make_async_remote_copy(
            src_ref=y_s.at[to], dst_ref=y_r.at[home],
            send_sem=y_ss.at[offset], recv_sem=y_rs.at[offset],
            device_id=(to, n), device_id_type=MESH,
        )

    def compute(to):
        applied = []
        for k in range(CAP):
            high, low = split(faces[shifted(word[k, to], 0, 6)])
            applied.append(dot(high, p_hi[...]) + dot(low, p_hi[...]) + dot(high, p_lo[...]))
        for k in range(CAP):
            s = to * CAP + k
            high, low = split(applied[k])
            both = dot(pt_hi[...], high) + dot(pt_lo[...], high) + dot(pt_hi[...], low)
            both = jnp.where(shifted(word[k, to], 21, 1) > 0, both[0:ROWS, :], 0.0)
            edge = both[:, 128:256]
            main_s[s] = both[:, 0:128]
            corner = pltpu.roll(edge[128:ROWS, :], 0, 1, stride=8, stride_axis=0)
            main_s[s, NC:ROWS, :] = jnp.sum(corner, axis=0, keepdims=True)
            rem_s[s] = edge[0:128, :].T[0:8, :]
            edge_s[s] = edge

    pl.semaphore_wait(barrier, WIDE + NARROW - 2)

    def spread(q, _):
        g_copy(q, zq).start()
        return 0

    lax.fori_loop(1, 16, spread, 0)
    words[...] = jnp.zeros_like(words)
    for i, row in enumerate(slot_words(elems, slots)):
        words[i : i + 1, :] = row
    fetch = pltpu.make_async_copy(words, word, word_sem)
    fetch.start()
    for i in range(5):
        load(i).wait()
    fetch.wait()

    def send(step, _):
        offset = offset_at(step)
        to = partner(offset, 1)
        compute(to)

        @pl.when((step < HELD) | (step == WIDE - 2))
        def _():
            main_copy(offset, to, w).start()
            rem_copy(offset, to, w).start()

        @pl.when(step == CORE_AT)
        def _():
            def arrive(q, _):
                home = (zq // 4 - q // 4 + 4) % 4 * 4 + (zq % 4 - q % 4 + 4) % 4
                g_copy(q, home).wait_recv()
                return 0

            lax.fori_loop(1, 16, arrive, 0)
            core_copy(core).start()

        @pl.when(step == NARROW_AT)
        def _():
            core_copy(1 - core).wait_recv()
            for i in range(1, NARROW):
                v_copy(i, n).start()

        return 0

    lax.fori_loop(0, WIDE, send, 0)
    mine = pl.ds(w * CAP, CAP)
    own_main = pltpu.make_async_copy(main_s.at[mine], main_o.at[mine], own_sem.at[0])
    own_rem = pltpu.make_async_copy(rem_s.at[mine], rem_o.at[mine], own_sem.at[1])
    own_main.start()
    own_rem.start()
    for i in range(1, NARROW):
        v_copy(i, (n + NARROW - i) % NARROW).wait_recv()

    def apply(to, _):
        for k in range(CAP):
            s = to * CAP + k
            row = pl.ds(shifted(word[k, to], 6, 3), 1)
            narrow = shifted(word[k, to], 9, 2)
            at = shifted(word[k, to], 11, 1) * 16 + shifted(word[k, to], 12, 4)
            head, tail = values[narrow, at, 0, row, :], values[narrow, at, 1, row, :]
            y = jnp.sum(main_s[s] * head + edge_s[s] * tail, axis=1, keepdims=True)
            label = shifted(word[k, to], 16, 5) * shifted(word[k, to], 21, 1) - 1 + shifted(word[k, to], 21, 1)
            y = jnp.where(sub == NC, label.astype(jnp.float32), y)
            sums[...] = jnp.where(lane == to * 4 + k, y, sums[...])
        return 0

    lax.fori_loop(0, WIDE, apply, 0)

    by_slot = jnp.concatenate([sums[0:128, :].T, jnp.pad(sums[128:ROWS, :].T, ((0, 0), (0, 120)))], axis=0)
    for to in range(WIDE):
        y_s[to, 0:3, :] = by_slot[4 * to : 4 * to + 3, :]
        y_s[to, 3:6, :] = by_slot[128 + 4 * to : 128 + 4 * to + 3, :]
        y_s[to, 6:8, :] = jnp.zeros((2, 128), jnp.float32)

    def send_y(offset, _):
        y_copy(offset, partner(offset, 1), w).start()
        return 0

    lax.fori_loop(1, WIDE, send_y, 0)
    y_r[w] = y_s[w]

    def send_held(step, _):
        offset = offset_at(step)
        to = partner(offset, 1)
        main_copy(offset, to, w).start()
        rem_copy(offset, to, w).start()
        return 0

    lax.fori_loop(HELD, WIDE - 2, send_held, 0)

    def wait_y(offset, _):
        y_copy(offset, partner(offset, 1), partner(offset, -1)).wait_recv()
        return 0

    lax.fori_loop(1, WIDE, wait_y, 0)

    terms = y_r[...].reshape(WIDE * 8, 128)
    labels = terms.T[7:8, :]
    place = lax.broadcasted_iota(jnp.int32, (OWN, WIDE * 8), 1) % 8
    of_row = lax.broadcasted_iota(jnp.int32, (OWN, WIDE * 8), 0).astype(jnp.float32)
    tail = jnp.where((labels == of_row) & (place >= 3) & (place < 6), 1.0, 0.0)
    head = pltpu.roll(tail, WIDE * 8 - 3, 1)
    head_sum = jnp.dot(head, terms, precision=PRECISE, preferred_element_type=jnp.float32)
    tail_sum = jnp.dot(tail, terms, precision=PRECISE, preferred_element_type=jnp.float32)
    for i in range(NARROW):
        x_s[i, 0:8, :] = head_sum[8 * i : 8 * i + 8, :]
        x_s[i, 8:16, :] = tail_sum[8 * i : 8 * i + 8, :]

    def x_copy(i, home):
        to = (n + i) % NARROW
        return pltpu.make_async_remote_copy(
            src_ref=x_s.at[to], dst_ref=x_r.at[home],
            send_sem=x_ss.at[i], recv_sem=x_rs.at[i],
            device_id=(w, to), device_id_type=MESH,
        )

    for i in range(1, NARROW):
        x_copy(i, n).start()
    x_r[n] = x_s[n]
    for i in range(1, NARROW):
        x_copy(i, (n + NARROW - i) % NARROW).wait_recv()
    total = x_r[0] + x_r[1] + x_r[2] + x_r[3]
    coupling = jnp.concatenate([total[0:8, :], total[8:16, :]], axis=1)[:, 0:NC]
    update = (1.0 - DAMPING) * rhs - coupling
    two = one + DAMPING * jacobi(inverse, update)
    fine_o[...] = jnp.dot(two, pt[...], precision=PRECISE, preferred_element_type=jnp.float32)

    def finish(offset, _):
        to, source = partner(offset, 1), partner(offset, -1)
        for copy in (main_copy, rem_copy):
            copy(offset, to, source).wait_recv()
        for copy in (main_copy, rem_copy, y_copy):
            copy(offset, to, w).wait_send()
        return 0

    lax.fori_loop(1, WIDE, finish, 0)

    def finish_spread(q, _):
        g_copy(q, zq).wait_send()
        return 0

    lax.fori_loop(1, 16, finish_spread, 0)
    core_copy(core).wait_send()
    for i in range(1, NARROW):
        x_copy(i, n).wait_send()
        v_copy(i, n).wait_send()
    own_main.wait()
    own_rem.wait()


def exchange(elems, slots, face_blocks, pt, residual, inverse):
    hbm = pl.BlockSpec(memory_space=pltpu.HBM)
    vmem = pl.BlockSpec(memory_space=pltpu.VMEM)
    anywhere = pl.BlockSpec(memory_space=pl.ANY)
    f32, bf16, dma = jnp.float32, jnp.bfloat16, pltpu.SemaphoreType.DMA
    return pl.pallas_call(
        exchange_kernel,
        out_shape=[
            jax.ShapeDtypeStruct((8, NF), f32),
            jax.ShapeDtypeStruct((SLOTS, ROWS, 128), f32),
            jax.ShapeDtypeStruct((SLOTS, 8, 128), f32),
        ],
        in_specs=[hbm] * 6,
        out_specs=[vmem, anywhere, anywhere],
        scratch_shapes=[
            pltpu.SMEM((2, FACES), jnp.int32),
            pltpu.SMEM((WIDE * OWN,), jnp.int32),
            pltpu.VMEM((8, 128), jnp.int32),
            pltpu.SMEM((8, 128), jnp.int32),
            pltpu.VMEM((NC, NF), f32),
            pltpu.VMEM((8, NF), f32),
            pltpu.VMEM((NC, 8, NC), f32),
            pltpu.VMEM((FACES, NF, NF), f32),
            pltpu.VMEM((256, NF), f32),
            pltpu.VMEM((NF, 256), bf16),
            pltpu.VMEM((NF, 256), bf16),
            pltpu.VMEM((144, NF), bf16),
            pltpu.VMEM((144, NF), bf16),
            pltpu.VMEM((SLOTS, ROWS, 128), f32),
            pltpu.VMEM((SLOTS, 8, 128), f32),
            pltpu.VMEM((SLOTS, ROWS, 128), f32),
            pltpu.VMEM((ROWS, 128), f32),
            pltpu.VMEM((WIDE, 8, 128), f32),
            pltpu.VMEM((WIDE, 8, 128), f32),
            pltpu.VMEM((NARROW, 16, 128), f32),
            pltpu.VMEM((NARROW, 16, 128), f32),
            pltpu.VMEM((NARROW, WIDE, 2, 8, 128), f32),
            dma((5,)),
            dma(()),
            dma((5,)),
        ]
        + [dma((WIDE,))] * 6
        + [dma((16,))] * 2
        + [dma((NARROW,))] * 4
        + [dma((2,))] * 2,
        compiler_params=pltpu.CompilerParams(
            collective_id=0, has_side_effects=True, vmem_limit_bytes=57600 << 10
        ),
        cost_estimate=pl.CostEstimate(flops=10**10, bytes_accessed=35 * 10**6, transcendentals=0),
        name="exchange",
    )(elems, slots, face_blocks, pt, residual, inverse)


def unpack_kernel(main_hbm, rem_hbm, fine_in, out, fine, edge, main, rem, sems):
    i = pl.program_id(0)
    rest = NC - 128

    def load(j):
        part = pl.ds(48 * j, min(48, ROWS - 48 * j))
        return pltpu.make_async_copy(
            main_hbm.at[:, part], main.reshape(SLOTS, ROWS, 128).at[:, part], sems.at[j]
        )

    load_rem = pltpu.make_async_copy(rem_hbm, rem, sems.at[3])

    def row(a):
        return main[pl.ds(a, SLOTS, stride=ROWS), :].T

    @pl.when(i == 0)
    def _():
        load(0).start()
        load_rem.start()
        load(1).start()
        load(2).start()
        fine[...] = fine_in[...]

    for j in range(NC // PART):

        @pl.when(i == j)
        def _(j=j):
            load(j).wait()
            for r in range(PART):
                out[r, 0:128, :] = row(j * PART + r)
            size = min(PART, 128 - j * PART)
            if j == 0:
                load_rem.wait()
                for c in range(rest):
                    edge[c] = rem[pl.ds(c, SLOTS, stride=8), :].T
            for c in range(rest):
                out[0:size, 128 + c, :] = edge[c, j * PART : j * PART + size, :]
            if size < PART:
                corner = row(NC)
                for r in range(rest):
                    out[size + r, 128:NC, :] = corner[8 * r : 8 * r + rest, :]


def unpack(main, rem, fine):
    vmem = pl.BlockSpec(memory_space=pltpu.VMEM)
    hbm = pl.BlockSpec(memory_space=pltpu.HBM)
    return pl.pallas_call(
        unpack_kernel,
        grid=(NC // PART,),
        out_shape=[
            jax.ShapeDtypeStruct((NC, NC, SLOTS), jnp.float32),
            jax.ShapeDtypeStruct((8, NF), jnp.float32),
        ],
        in_specs=[hbm, hbm, vmem],
        out_specs=[
            pl.BlockSpec((PART, NC, SLOTS), lambda i: (i, 0, 0)),
            pl.BlockSpec((8, NF), lambda i: (0, 0)),
        ],
        scratch_shapes=[
            pltpu.VMEM((NC - 128, 128, SLOTS), jnp.float32),
            pltpu.VMEM((SLOTS * ROWS, 128), jnp.float32),
            pltpu.VMEM((SLOTS * 8, 128), jnp.float32),
            pltpu.SemaphoreType.DMA((4,)),
        ],
        compiler_params=pltpu.CompilerParams(vmem_limit_bytes=57600 << 10),
        name="unpack",
    )(main, rem, fine)


def local(face_blocks, face_elems, coarse_slot, prolong, fine_residual, block_inverse):
    fine, main, rem = exchange(
        face_elems.T, coarse_slot, face_blocks, prolong.T, fine_residual, jnp.transpose(block_inverse, (1, 0, 2))
    )
    owned, fine = unpack(main, rem.reshape(SLOTS * 8, 128), fine)
    return fine, jnp.transpose(owned, (2, 0, 1))


def solution(mesh):
    placed = (
        P(("wide", "narrow"), None, None),
        P(("wide", "narrow"), None),
        P(),
        P(),
        P(("wide", "narrow"), None),
        P(("wide", "narrow"), None, None),
    )
    return jax.shard_map(
        local,
        mesh=mesh,
        in_specs=placed,
        out_specs=(P(("wide", "narrow"), None), P(("wide", "narrow"), None, None)),
        check_vma=False,
    )
```

```python
import functools

import jax
import jax.numpy as jnp
from jax import lax
from jax.experimental import pallas as pl
from jax.experimental.pallas import tpu as pltpu
from jax.sharding import PartitionSpec as P

DAMPING = 0.7
PRECISE = lax.Precision.HIGHEST
MESH = pl.DeviceIdType.MESH

NF = 320
NC = 135
ROWS = 136
PART = 27
CUTS = (0, 32, 56, 88, 112, ROWS)
FACES = 40
WIDE = 32
NARROW = 4
CAP = 3
SLOTS = WIDE * CAP
OWN = 32
PAIRS = (
    (1, 1), (3, 3), (1, 3), (3, 1), (2, 1), (0, 3), (2, 3), (0, 1),
    (1, 2), (3, 0), (3, 2), (1, 0), (2, 0), (0, 2), (2, 2),
)
CODES = tuple(
    sum((4 * dz + dy) * 16**i for i, (dz, dy) in enumerate(PAIRS[at : at + 7])) for at in (0, 7, 14)
)
CORE_AT, NARROW_AT = 2, 5
HELD = 26


def offset_at(step):
    last, near = step // 28, step // 30
    pair = (step // 4 * 2 + step % 2) * (1 - last) + 14 * last
    core = step // 2 % 2 * (1 - last) + (step - 28) * last
    part = pair // 7
    first, second, third = (part - 1) * (part - 2) // 2, part * (2 - part), part * (part - 1) // 2
    code = CODES[0] * first + CODES[1] * second + CODES[2] * third
    offset = lax.shift_right_logical(code, 4 * (pair % 7)) % 16 * 2 + core
    return offset * (1 - near) + (31 - step) * near


def slot_words(faces, slots):
    lane = lax.broadcasted_iota(jnp.int32, (1, 128), 1)

    def place(f, words):
        first, second, third = words
        row = slots[faces[0, f]]
        word = (1 << 21) + (row & (OWN - 1)) * 65536 + slots[faces[1, f]] * 64 + f
        here = lane == lax.shift_right_logical(row, 5)
        third = jnp.where(here & (second > 0), word, third)
        second = jnp.where(here & (first > 0) & (second == 0), word, second)
        first = jnp.where(here & (first == 0), word, first)
        return first, second, third

    empty = jnp.zeros((1, 128), jnp.int32)
    return lax.fori_loop(0, FACES, place, (empty, empty, empty), unroll=4)


def shifted(word, by, bits):
    return lax.shift_right_logical(word, by) & ((1 << bits) - 1)


def split(x):
    high = x.astype(jnp.bfloat16)
    return high, (x - high.astype(jnp.float32)).astype(jnp.bfloat16)


def dot(a, b):
    return jnp.dot(a, b, preferred_element_type=jnp.float32)


def dot_t(a, b):
    return lax.dot_general(
        a, b, (((1,), (1,)), ((), ())), precision=PRECISE, preferred_element_type=jnp.float32
    )


def jacobi(inverse, vectors):
    row = lax.broadcasted_iota(jnp.int32, (8, NC), 0)
    out = jnp.zeros((8, NC), jnp.float32)
    for s in range(8):
        out = jnp.where(row == s, dot_t(vectors, inverse[:, s, :]), out)
    return out


def exchange_kernel(
    elems_hbm, slots_hbm, faces_hbm, pt_hbm, residual_hbm, inverse_hbm,
    fine_o, main_o, rem_o,
    elems, slots, words, word, pt, residual, inverse, faces, wide_pt, p_hi, p_lo, pt_hi, pt_lo, main_s, rem_s, edge_s, sums, y_s, y_r, x_s, x_r,
    values,
    in_sem, word_sem, face_sem, main_ss, main_rs, rem_ss, rem_rs, y_ss, y_rs, g_ss, g_rs, x_ss, x_rs, v_ss, v_rs,
    core_sem, own_sem,
):
    w = lax.axis_index("wide")
    n = lax.axis_index("narrow")

    def load(i):
        part = pl.ds(i * 8, 8)
        return pltpu.make_async_copy(faces_hbm.at[part], faces.at[part], face_sem.at[i])

    inputs = [
        pltpu.make_async_copy(source, target, in_sem.at[i])
        for i, (source, target) in enumerate(
            ((elems_hbm, elems), (slots_hbm, slots), (pt_hbm, pt), (residual_hbm, residual), (inverse_hbm, inverse))
        )
    ]
    for copy in inputs:
        copy.start()
    for i in range(5):
        load(i).start()

    def partner(offset, sign):
        z, y, c = w // 8, (w // 2) % 4, w % 2
        dz, dy, dc = offset // 8, (offset // 2) % 4, offset % 2
        return ((z + sign * dz + 4) % 4) * 8 + ((y + sign * dy + 4) % 4) * 2 + (c + dc) % 2

    barrier = pltpu.get_barrier_semaphore()

    def greet(i, _):
        pl.semaphore_signal(barrier, inc=1, device_id=(partner(i, 1), n), device_id_type=MESH)
        return 0

    lax.fori_loop(1, WIDE, greet, 0)
    for i in range(1, NARROW):
        pl.semaphore_signal(barrier, inc=1, device_id=(w, (n + i) % NARROW), device_id_type=MESH)

    for copy in inputs[0:2]:
        copy.wait()
    words[...] = jnp.zeros_like(words)
    for i, row in enumerate(slot_words(elems, slots)):
        words[i : i + 1, :] = row
    fetch = pltpu.make_async_copy(words, word, word_sem)
    fetch.start()
    for copy in inputs[2:5]:
        copy.wait()
    wide_pt[...] = jnp.zeros_like(wide_pt)
    wide_pt[0:NC, :] = pt[...]
    pt_hi[...], pt_lo[...] = split(wide_pt[0:144, :])
    p_hi[...], p_lo[...] = split(wide_pt[...].T)

    rhs = dot_t(residual[...], pt[...])
    one = DAMPING * jacobi(inverse, rhs)
    zq, core = w // 2, w % 2
    values[n, core * 16 + zq, 0] = one[:, 0:128]
    values[n, core * 16 + zq, 1] = jnp.pad(one[:, 128:NC], ((0, 0), (0, 256 - NC)))

    def v_copy(i, home):
        return pltpu.make_async_remote_copy(
            src_ref=values.at[n], dst_ref=values.at[home], send_sem=v_ss.at[i], recv_sem=v_rs.at[i],
            device_id=(w, (n + i) % NARROW), device_id_type=MESH,
        )

    def g_copy(q, home):
        chip = (zq // 4 + q // 4) % 4 * 4 + (zq % 4 + q % 4) % 4
        return pltpu.make_async_remote_copy(
            src_ref=values.at[n, core * 16 + zq], dst_ref=values.at[n, core * 16 + home],
            send_sem=g_ss.at[q], recv_sem=g_rs.at[q],
            device_id=(chip * 2 + core, n), device_id_type=MESH,
        )

    def core_copy(half):
        part = pl.ds(half * 16, 16)
        return pltpu.make_async_remote_copy(
            src_ref=values.at[n, part], dst_ref=values.at[n, part],
            send_sem=core_sem.at[0], recv_sem=core_sem.at[1],
            device_id=(zq * 2 + 1 - core, n), device_id_type=MESH,
        )

    lane = lax.broadcasted_iota(jnp.int32, (ROWS, 128), 1)
    sub = lax.broadcasted_iota(jnp.int32, (ROWS, 1), 0)
    sums[...] = jnp.where(lax.broadcasted_iota(jnp.int32, (ROWS, 128), 0) == NC, -1.0, 0.0)

    def main_copy(offset, to, home):
        return pltpu.make_async_remote_copy(
            src_ref=main_s.at[pl.ds(to * CAP, CAP)],
            dst_ref=main_o.at[pl.ds(home * CAP, CAP)],
            send_sem=main_ss.at[offset], recv_sem=main_rs.at[offset],
            device_id=(to, n), device_id_type=MESH,
        )

    def rem_copy(offset, to, home):
        return pltpu.make_async_remote_copy(
            src_ref=rem_s.at[pl.ds(to * CAP, CAP)],
            dst_ref=rem_o.at[pl.ds(home * CAP, CAP)],
            send_sem=rem_ss.at[offset], recv_sem=rem_rs.at[offset],
            device_id=(to, n), device_id_type=MESH,
        )

    def y_copy(offset, to, home):
        return pltpu.make_async_remote_copy(
            src_ref=y_s.at[to], dst_ref=y_r.at[home],
            send_sem=y_ss.at[offset], recv_sem=y_rs.at[offset],
            device_id=(to, n), device_id_type=MESH,
        )

    def compute(to):
        applied = []
        for k in range(CAP):
            high, low = split(faces[shifted(word[k, to], 0, 6)])
            applied.append(dot(high, p_hi[...]) + dot(low, p_hi[...]) + dot(high, p_lo[...]))
        for k in range(CAP):
            s = to * CAP + k
            high, low = split(applied[k])
            both = dot(pt_hi[...], high) + dot(pt_lo[...], high) + dot(pt_hi[...], low)
            both = jnp.where(shifted(word[k, to], 21, 1) > 0, both[0:ROWS, :], 0.0)
            edge = both[:, 128:256]
            main_s[s] = both[:, 0:128]
            corner = pltpu.roll(edge[128:ROWS, :], 0, 1, stride=8, stride_axis=0)
            main_s[s, NC:ROWS, :] = jnp.sum(corner, axis=0, keepdims=True)
            rem_s[s] = edge[0:128, :].T[0:8, :]
            edge_s[s] = edge

    pl.semaphore_wait(barrier, WIDE + NARROW - 2)

    def spread(q, _):
        g_copy(q, zq).start()
        return 0

    lax.fori_loop(1, 16, spread, 0)
    for i in range(5):
        load(i).wait()
    fetch.wait()

    def send(step, _):
        offset = offset_at(step)
        to = partner(offset, 1)
        compute(to)

        @pl.when((step < HELD) | (step == WIDE - 2))
        def _():
            main_copy(offset, to, w).start()
            rem_copy(offset, to, w).start()

        @pl.when(step == CORE_AT)
        def _():
            def arrive(q, _):
                home = (zq // 4 - q // 4 + 4) % 4 * 4 + (zq % 4 - q % 4 + 4) % 4
                g_copy(q, home).wait_recv()
                return 0

            lax.fori_loop(1, 16, arrive, 0)
            core_copy(core).start()

        @pl.when(step == NARROW_AT)
        def _():
            core_copy(1 - core).wait_recv()
            for i in range(1, NARROW):
                v_copy(i, n).start()

        return 0

    lax.fori_loop(0, WIDE, send, 0)
    mine = pl.ds(w * CAP, CAP)
    own_main = pltpu.make_async_copy(main_s.at[mine], main_o.at[mine], own_sem.at[0])
    own_rem = pltpu.make_async_copy(rem_s.at[mine], rem_o.at[mine], own_sem.at[1])
    own_main.start()
    own_rem.start()
    for i in range(1, NARROW):
        v_copy(i, (n + NARROW - i) % NARROW).wait_recv()

    def apply(to, _):
        for k in range(CAP):
            s = to * CAP + k
            row = pl.ds(shifted(word[k, to], 6, 3), 1)
            narrow = shifted(word[k, to], 9, 2)
            at = shifted(word[k, to], 11, 1) * 16 + shifted(word[k, to], 12, 4)
            head, tail = values[narrow, at, 0, row, :], values[narrow, at, 1, row, :]
            y = jnp.sum(main_s[s] * head + edge_s[s] * tail, axis=1, keepdims=True)
            label = shifted(word[k, to], 16, 5) * shifted(word[k, to], 21, 1) - 1 + shifted(word[k, to], 21, 1)
            y = jnp.where(sub == NC, label.astype(jnp.float32), y)
            sums[...] = jnp.where(lane == to * 4 + k, y, sums[...])
        return 0

    lax.fori_loop(0, WIDE, apply, 0)

    by_slot = jnp.concatenate([sums[0:128, :].T, jnp.pad(sums[128:ROWS, :].T, ((0, 0), (0, 120)))], axis=0)
    for to in range(WIDE):
        y_s[to, 0:3, :] = by_slot[4 * to : 4 * to + 3, :]
        y_s[to, 3:6, :] = by_slot[128 + 4 * to : 128 + 4 * to + 3, :]
        y_s[to, 6:8, :] = jnp.zeros((2, 128), jnp.float32)

    def send_y(offset, _):
        y_copy(offset, partner(offset, 1), w).start()
        return 0

    lax.fori_loop(1, WIDE, send_y, 0)
    y_r[w] = y_s[w]

    def send_held(step, _):
        offset = offset_at(step)
        to = partner(offset, 1)
        main_copy(offset, to, w).start()
        rem_copy(offset, to, w).start()
        return 0

    lax.fori_loop(HELD, WIDE - 2, send_held, 0)

    def wait_y(offset, _):
        y_copy(offset, partner(offset, 1), partner(offset, -1)).wait_recv()
        return 0

    lax.fori_loop(1, WIDE, wait_y, 0)

    terms = y_r[...].reshape(WIDE * 8, 128)
    labels = terms.T[7:8, :]
    place = lax.broadcasted_iota(jnp.int32, (OWN, WIDE * 8), 1) % 8
    of_row = lax.broadcasted_iota(jnp.int32, (OWN, WIDE * 8), 0).astype(jnp.float32)
    tail = jnp.where((labels == of_row) & (place >= 3) & (place < 6), 1.0, 0.0)
    head = pltpu.roll(tail, WIDE * 8 - 3, 1)
    head_sum = jnp.dot(head, terms, precision=PRECISE, preferred_element_type=jnp.float32)
    tail_sum = jnp.dot(tail, terms, precision=PRECISE, preferred_element_type=jnp.float32)
    for i in range(NARROW):
        x_s[i, 0:8, :] = head_sum[8 * i : 8 * i + 8, :]
        x_s[i, 8:16, :] = tail_sum[8 * i : 8 * i + 8, :]

    def x_copy(i, home):
        to = (n + i) % NARROW
        return pltpu.make_async_remote_copy(
            src_ref=x_s.at[to], dst_ref=x_r.at[home],
            send_sem=x_ss.at[i], recv_sem=x_rs.at[i],
            device_id=(w, to), device_id_type=MESH,
        )

    for i in range(1, NARROW):
        x_copy(i, n).start()
    x_r[n] = x_s[n]
    for i in range(1, NARROW):
        x_copy(i, (n + NARROW - i) % NARROW).wait_recv()
    total = x_r[0] + x_r[1] + x_r[2] + x_r[3]
    coupling = jnp.concatenate([total[0:8, :], total[8:16, :]], axis=1)[:, 0:NC]
    update = (1.0 - DAMPING) * rhs - coupling
    two = one + DAMPING * jacobi(inverse, update)
    fine_o[...] = jnp.dot(two, pt[...], precision=PRECISE, preferred_element_type=jnp.float32)

    def finish(offset, _):
        to, source = partner(offset, 1), partner(offset, -1)
        for copy in (main_copy, rem_copy):
            copy(offset, to, source).wait_recv()
        for copy in (main_copy, rem_copy, y_copy):
            copy(offset, to, w).wait_send()
        return 0

    lax.fori_loop(1, WIDE, finish, 0)

    def finish_spread(q, _):
        g_copy(q, zq).wait_send()
        return 0

    lax.fori_loop(1, 16, finish_spread, 0)
    core_copy(core).wait_send()
    for i in range(1, NARROW):
        x_copy(i, n).wait_send()
        v_copy(i, n).wait_send()
    own_main.wait()
    own_rem.wait()


def exchange(elems, slots, face_blocks, pt, residual, inverse):
    hbm = pl.BlockSpec(memory_space=pltpu.HBM)
    vmem = pl.BlockSpec(memory_space=pltpu.VMEM)
    anywhere = pl.BlockSpec(memory_space=pl.ANY)
    f32, bf16, dma = jnp.float32, jnp.bfloat16, pltpu.SemaphoreType.DMA
    return pl.pallas_call(
        exchange_kernel,
        out_shape=[
            jax.ShapeDtypeStruct((8, NF), f32),
            jax.ShapeDtypeStruct((SLOTS, ROWS, 128), f32),
            jax.ShapeDtypeStruct((SLOTS, 8, 128), f32),
        ],
        in_specs=[hbm] * 6,
        out_specs=[vmem, anywhere, anywhere],
        scratch_shapes=[
            pltpu.SMEM((2, FACES), jnp.int32),
            pltpu.SMEM((WIDE * OWN,), jnp.int32),
            pltpu.VMEM((8, 128), jnp.int32),
            pltpu.SMEM((8, 128), jnp.int32),
            pltpu.VMEM((NC, NF), f32),
            pltpu.VMEM((8, NF), f32),
            pltpu.VMEM((NC, 8, NC), f32),
            pltpu.VMEM((FACES, NF, NF), f32),
            pltpu.VMEM((256, NF), f32),
            pltpu.VMEM((NF, 256), bf16),
            pltpu.VMEM((NF, 256), bf16),
            pltpu.VMEM((144, NF), bf16),
            pltpu.VMEM((144, NF), bf16),
            pltpu.VMEM((SLOTS, ROWS, 128), f32),
            pltpu.VMEM((SLOTS, 8, 128), f32),
            pltpu.VMEM((SLOTS, ROWS, 128), f32),
            pltpu.VMEM((ROWS, 128), f32),
            pltpu.VMEM((WIDE, 8, 128), f32),
            pltpu.VMEM((WIDE, 8, 128), f32),
            pltpu.VMEM((NARROW, 16, 128), f32),
            pltpu.VMEM((NARROW, 16, 128), f32),
            pltpu.VMEM((NARROW, WIDE, 2, 8, 128), f32),
            dma((5,)),
            dma(()),
            dma((5,)),
        ]
        + [dma((WIDE,))] * 6
        + [dma((16,))] * 2
        + [dma((NARROW,))] * 4
        + [dma((2,))] * 2,
        compiler_params=pltpu.CompilerParams(
            collective_id=0, has_side_effects=True, vmem_limit_bytes=57600 << 10
        ),
        cost_estimate=pl.CostEstimate(flops=10**10, bytes_accessed=35 * 10**6, transcendentals=0),
        name="exchange",
    )(elems, slots, face_blocks, pt, residual, inverse)


def unpack_kernel(main_hbm, rem_hbm, fine_in, out, fine, edge, main, rem, sems):
    i = pl.program_id(0)
    rest = NC - 128

    def load(j):
        part = pl.ds(CUTS[j], CUTS[j + 1] - CUTS[j])
        return pltpu.make_async_copy(
            main_hbm.at[:, part], main.reshape(SLOTS, ROWS, 128).at[:, part], sems.at[j]
        )

    load_rem = pltpu.make_async_copy(rem_hbm, rem, sems.at[5])

    def row(a):
        return main[pl.ds(a, SLOTS, stride=ROWS), :].T

    @pl.when(i == 0)
    def _():
        load(0).start()
        load_rem.start()
        for j in range(1, NC // PART):
            load(j).start()
        fine[...] = fine_in[...]

    for j in range(NC // PART):

        @pl.when(i == j)
        def _(j=j):
            load(j).wait()
            for r in range(PART):
                out[r, 0:128, :] = row(j * PART + r)
            size = min(PART, 128 - PART * j)
            if j == 0:
                load_rem.wait()
                for c in range(rest):
                    edge[c] = rem[pl.ds(c, SLOTS, stride=8), :].T
            for c in range(rest):
                out[0:size, 128 + c, :] = edge[c, j * PART : j * PART + size, :]
            if size < PART:
                corner = row(NC)
                for r in range(rest):
                    out[size + r, 128:NC, :] = corner[8 * r : 8 * r + rest, :]


def unpack(main, rem, fine):
    vmem = pl.BlockSpec(memory_space=pltpu.VMEM)
    hbm = pl.BlockSpec(memory_space=pltpu.HBM)
    return pl.pallas_call(
        unpack_kernel,
        grid=(NC // PART,),
        out_shape=[
            jax.ShapeDtypeStruct((NC, NC, SLOTS), jnp.float32),
            jax.ShapeDtypeStruct((8, NF), jnp.float32),
        ],
        in_specs=[hbm, hbm, vmem],
        out_specs=[
            pl.BlockSpec((PART, NC, SLOTS), lambda i: (i, 0, 0)),
            pl.BlockSpec((8, NF), lambda i: (0, 0)),
        ],
        scratch_shapes=[
            pltpu.VMEM((NC - 128, 128, SLOTS), jnp.float32),
            pltpu.VMEM((SLOTS * ROWS, 128), jnp.float32),
            pltpu.VMEM((SLOTS * 8, 128), jnp.float32),
            pltpu.SemaphoreType.DMA((6,)),
        ],
        compiler_params=pltpu.CompilerParams(vmem_limit_bytes=57600 << 10),
        name="unpack",
    )(main, rem, fine)


def local(face_blocks, face_elems, coarse_slot, prolong, fine_residual, block_inverse):
    fine, main, rem = exchange(
        face_elems.T, coarse_slot, face_blocks, prolong.T, fine_residual, jnp.transpose(block_inverse, (1, 0, 2))
    )
    owned, fine = unpack(main, rem.reshape(SLOTS * 8, 128), fine)
    return fine, jnp.transpose(owned, (2, 0, 1))


def solution(mesh):
    placed = (
        P(("wide", "narrow"), None, None),
        P(("wide", "narrow"), None),
        P(),
        P(),
        P(("wide", "narrow"), None),
        P(("wide", "narrow"), None, None),
    )
    return jax.shard_map(
        local,
        mesh=mesh,
        in_specs=placed,
        out_specs=(P(("wide", "narrow"), None), P(("wide", "narrow"), None, None)),
        check_vma=False,
    )
```

```python
import functools

import jax
import jax.numpy as jnp
from jax import lax
from jax.experimental import pallas as pl
from jax.experimental.pallas import tpu as pltpu
from jax.sharding import PartitionSpec as P

DAMPING = 0.7
PRECISE = lax.Precision.HIGHEST
MESH = pl.DeviceIdType.MESH

NF = 320
NC = 135
ROWS = 136
PART = 45
FACES = 40
WIDE = 32
NARROW = 4
CAP = 3
SLOTS = WIDE * CAP
OWN = 32
PAIRS = (
    (1, 1), (3, 3), (1, 3), (3, 1), (2, 1), (0, 3), (2, 3), (0, 1),
    (1, 2), (3, 0), (3, 2), (1, 0), (2, 0), (0, 2), (2, 2),
)
CODES = tuple(
    sum((4 * dz + dy) * 16**i for i, (dz, dy) in enumerate(PAIRS[at : at + 7])) for at in (0, 7, 14)
)
CORE_AT, NARROW_AT = 2, 5
HELD = 26


def offset_at(step):
    last, near = step // 28, step // 30
    pair = (step // 4 * 2 + step % 2) * (1 - last) + 14 * last
    core = step // 2 % 2 * (1 - last) + (step - 28) * last
    part = pair // 7
    first, second, third = (part - 1) * (part - 2) // 2, part * (2 - part), part * (part - 1) // 2
    code = CODES[0] * first + CODES[1] * second + CODES[2] * third
    offset = lax.shift_right_logical(code, 4 * (pair % 7)) % 16 * 2 + core
    return offset * (1 - near) + (31 - step) * near


def slot_words(faces, slots):
    lane = lax.broadcasted_iota(jnp.int32, (1, 128), 1)

    def place(f, words):
        first, second, third = words
        row = slots[faces[0, f]]
        word = (1 << 21) + (row & (OWN - 1)) * 65536 + slots[faces[1, f]] * 64 + f
        here = lane == lax.shift_right_logical(row, 5)
        third = jnp.where(here & (second > 0), word, third)
        second = jnp.where(here & (first > 0) & (second == 0), word, second)
        first = jnp.where(here & (first == 0), word, first)
        return first, second, third

    empty = jnp.zeros((1, 128), jnp.int32)
    return lax.fori_loop(0, FACES, place, (empty, empty, empty), unroll=4)


def shifted(word, by, bits):
    return lax.shift_right_logical(word, by) & ((1 << bits) - 1)


def split(x):
    high = x.astype(jnp.bfloat16)
    return high, (x - high.astype(jnp.float32)).astype(jnp.bfloat16)


def dot(a, b):
    return jnp.dot(a, b, preferred_element_type=jnp.float32)


def dot_t(a, b):
    return lax.dot_general(
        a, b, (((1,), (1,)), ((), ())), precision=PRECISE, preferred_element_type=jnp.float32
    )


def jacobi(inverse, vectors):
    row = lax.broadcasted_iota(jnp.int32, (8, NC), 0)
    out = jnp.zeros((8, NC), jnp.float32)
    for s in range(8):
        out = jnp.where(row == s, dot_t(vectors, inverse[:, s, :]), out)
    return out


def exchange_kernel(
    elems_hbm, slots_hbm, faces_hbm, pt_hbm, residual_hbm, inverse_hbm,
    fine_o, main_o, rem_o,
    elems, slots, words, word, pt, residual, inverse, faces, wide_pt, p_hi, p_lo, pt_hi, pt_lo, main_s, rem_s, edge_s, sums, y_s, y_r, x_s, x_r,
    values,
    in_sem, word_sem, face_sem, main_ss, main_rs, rem_ss, rem_rs, y_ss, y_rs, g_ss, g_rs, x_ss, x_rs, v_ss, v_rs,
    core_sem, own_sem,
):
    w = lax.axis_index("wide")
    n = lax.axis_index("narrow")

    def load(i):
        part = pl.ds(i * 8, 8)
        return pltpu.make_async_copy(faces_hbm.at[part], faces.at[part], face_sem.at[i])

    inputs = [
        pltpu.make_async_copy(source, target, in_sem.at[i])
        for i, (source, target) in enumerate(
            ((elems_hbm, elems), (slots_hbm, slots), (pt_hbm, pt), (residual_hbm, residual), (inverse_hbm, inverse))
        )
    ]
    for copy in inputs:
        copy.start()
    for i in range(5):
        load(i).start()

    def partner(offset, sign):
        z, y, c = w // 8, (w // 2) % 4, w % 2
        dz, dy, dc = offset // 8, (offset // 2) % 4, offset % 2
        return ((z + sign * dz + 4) % 4) * 8 + ((y + sign * dy + 4) % 4) * 2 + (c + dc) % 2

    barrier = pltpu.get_barrier_semaphore()

    def greet(i, _):
        pl.semaphore_signal(barrier, inc=1, device_id=(partner(i, 1), n), device_id_type=MESH)
        return 0

    lax.fori_loop(1, WIDE, greet, 0)
    for i in range(1, NARROW):
        pl.semaphore_signal(barrier, inc=1, device_id=(w, (n + i) % NARROW), device_id_type=MESH)

    for copy in inputs[0:2]:
        copy.wait()
    words[...] = jnp.zeros_like(words)
    for i, row in enumerate(slot_words(elems, slots)):
        words[i : i + 1, :] = row
    fetch = pltpu.make_async_copy(words, word, word_sem)
    fetch.start()
    for copy in inputs[2:5]:
        copy.wait()
    wide_pt[...] = jnp.zeros_like(wide_pt)
    wide_pt[0:NC, :] = pt[...]
    pt_hi[...], pt_lo[...] = split(wide_pt[0:144, :])
    p_hi[...], p_lo[...] = split(wide_pt[...].T)

    rhs = dot_t(residual[...], pt[...])
    one = DAMPING * jacobi(inverse, rhs)
    zq, core = w // 2, w % 2
    values[n, core * 16 + zq, 0] = one[:, 0:128]
    values[n, core * 16 + zq, 1] = jnp.pad(one[:, 128:NC], ((0, 0), (0, 256 - NC)))

    def v_copy(i, home):
        return pltpu.make_async_remote_copy(
            src_ref=values.at[n], dst_ref=values.at[home], send_sem=v_ss.at[i], recv_sem=v_rs.at[i],
            device_id=(w, (n + i) % NARROW), device_id_type=MESH,
        )

    def g_copy(q, home):
        chip = (zq // 4 + q // 4) % 4 * 4 + (zq % 4 + q % 4) % 4
        return pltpu.make_async_remote_copy(
            src_ref=values.at[n, core * 16 + zq], dst_ref=values.at[n, core * 16 + home],
            send_sem=g_ss.at[q], recv_sem=g_rs.at[q],
            device_id=(chip * 2 + core, n), device_id_type=MESH,
        )

    def core_copy(half):
        part = pl.ds(half * 16, 16)
        return pltpu.make_async_remote_copy(
            src_ref=values.at[n, part], dst_ref=values.at[n, part],
            send_sem=core_sem.at[0], recv_sem=core_sem.at[1],
            device_id=(zq * 2 + 1 - core, n), device_id_type=MESH,
        )

    lane = lax.broadcasted_iota(jnp.int32, (ROWS, 128), 1)
    sub = lax.broadcasted_iota(jnp.int32, (ROWS, 1), 0)
    sums[...] = jnp.where(lax.broadcasted_iota(jnp.int32, (ROWS, 128), 0) == NC, -1.0, 0.0)

    def main_copy(offset, to, home):
        return pltpu.make_async_remote_copy(
            src_ref=main_s.at[pl.ds(to * CAP, CAP)],
            dst_ref=main_o.at[pl.ds(home * CAP, CAP)],
            send_sem=main_ss.at[offset], recv_sem=main_rs.at[offset],
            device_id=(to, n), device_id_type=MESH,
        )

    def rem_copy(offset, to, home):
        return pltpu.make_async_remote_copy(
            src_ref=rem_s.at[pl.ds(to * CAP, CAP)],
            dst_ref=rem_o.at[pl.ds(home * CAP, CAP)],
            send_sem=rem_ss.at[offset], recv_sem=rem_rs.at[offset],
            device_id=(to, n), device_id_type=MESH,
        )

    def y_copy(offset, to, home):
        return pltpu.make_async_remote_copy(
            src_ref=y_s.at[to], dst_ref=y_r.at[home],
            send_sem=y_ss.at[offset], recv_sem=y_rs.at[offset],
            device_id=(to, n), device_id_type=MESH,
        )

    def compute(to):
        applied = []
        for k in range(CAP):
            high, low = split(faces[shifted(word[k, to], 0, 6)])
            applied.append(dot(high, p_hi[...]) + dot(low, p_hi[...]) + dot(high, p_lo[...]))
        for k in range(CAP):
            s = to * CAP + k
            high, low = split(applied[k])
            both = dot(pt_hi[...], high) + dot(pt_lo[...], high) + dot(pt_hi[...], low)
            both = jnp.where(shifted(word[k, to], 21, 1) > 0, both[0:ROWS, :], 0.0)
            edge = both[:, 128:256]
            main_s[s] = both[:, 0:128]
            corner = pltpu.roll(edge[128:ROWS, :], 0, 1, stride=8, stride_axis=0)
            main_s[s, NC:ROWS, :] = jnp.sum(corner, axis=0, keepdims=True)
            rem_s[s] = edge[0:128, :].T[0:8, :]
            edge_s[s] = edge

    pl.semaphore_wait(barrier, WIDE + NARROW - 2)

    def spread(q, _):
        g_copy(q, zq).start()
        return 0

    lax.fori_loop(1, 16, spread, 0)
    for i in range(5):
        load(i).wait()
    fetch.wait()

    def send(step, _):
        offset = offset_at(step)
        to = partner(offset, 1)
        compute(to)

        @pl.when((step < HELD) | (step == WIDE - 2))
        def _():
            main_copy(offset, to, w).start()
            rem_copy(offset, to, w).start()

        @pl.when(step == CORE_AT)
        def _():
            def arrive(q, _):
                home = (zq // 4 - q // 4 + 4) % 4 * 4 + (zq % 4 - q % 4 + 4) % 4
                g_copy(q, home).wait_recv()
                return 0

            lax.fori_loop(1, 16, arrive, 0)
            core_copy(core).start()

        @pl.when(step == NARROW_AT)
        def _():
            core_copy(1 - core).wait_recv()
            for i in range(1, NARROW):
                v_copy(i, n).start()

        return 0

    lax.fori_loop(0, WIDE, send, 0)
    mine = pl.ds(w * CAP, CAP)
    own_main = pltpu.make_async_copy(main_s.at[mine], main_o.at[mine], own_sem.at[0])
    own_rem = pltpu.make_async_copy(rem_s.at[mine], rem_o.at[mine], own_sem.at[1])
    own_main.start()
    own_rem.start()
    for i in range(1, NARROW):
        v_copy(i, (n + NARROW - i) % NARROW).wait_recv()

    def apply(to, _):
        for k in range(CAP):
            s = to * CAP + k
            row = pl.ds(shifted(word[k, to], 6, 3), 1)
            narrow = shifted(word[k, to], 9, 2)
            at = shifted(word[k, to], 11, 1) * 16 + shifted(word[k, to], 12, 4)
            head, tail = values[narrow, at, 0, row, :], values[narrow, at, 1, row, :]
            y = jnp.sum(main_s[s] * head + edge_s[s] * tail, axis=1, keepdims=True)
            label = shifted(word[k, to], 16, 5) * shifted(word[k, to], 21, 1) - 1 + shifted(word[k, to], 21, 1)
            y = jnp.where(sub == NC, label.astype(jnp.float32), y)
            sums[...] = jnp.where(lane == to * 4 + k, y, sums[...])
        return 0

    lax.fori_loop(0, WIDE, apply, 0)

    by_slot = jnp.concatenate([sums[0:128, :].T, jnp.pad(sums[128:ROWS, :].T, ((0, 0), (0, 120)))], axis=0)
    for to in range(WIDE):
        y_s[to, 0:3, :] = by_slot[4 * to : 4 * to + 3, :]
        y_s[to, 3:6, :] = by_slot[128 + 4 * to : 128 + 4 * to + 3, :]
        y_s[to, 6:8, :] = jnp.zeros((2, 128), jnp.float32)

    def send_y(offset, _):
        y_copy(offset, partner(offset, 1), w).start()
        return 0

    lax.fori_loop(1, WIDE, send_y, 0)
    y_r[w] = y_s[w]

    def send_held(step, _):
        offset = offset_at(step)
        to = partner(offset, 1)
        main_copy(offset, to, w).start()
        rem_copy(offset, to, w).start()
        return 0

    lax.fori_loop(HELD, WIDE - 2, send_held, 0)

    def wait_y(offset, _):
        y_copy(offset, partner(offset, 1), partner(offset, -1)).wait_recv()
        return 0

    lax.fori_loop(1, WIDE, wait_y, 0)

    terms = y_r[...].reshape(WIDE * 8, 128)
    labels = terms.T[7:8, :]
    place = lax.broadcasted_iota(jnp.int32, (OWN, WIDE * 8), 1) % 8
    of_row = lax.broadcasted_iota(jnp.int32, (OWN, WIDE * 8), 0).astype(jnp.float32)
    tail = jnp.where((labels == of_row) & (place >= 3) & (place < 6), 1.0, 0.0)
    head = pltpu.roll(tail, WIDE * 8 - 3, 1)
    head_sum = jnp.dot(head, terms, precision=PRECISE, preferred_element_type=jnp.float32)
    tail_sum = jnp.dot(tail, terms, precision=PRECISE, preferred_element_type=jnp.float32)
    for i in range(NARROW):
        x_s[i, 0:8, :] = head_sum[8 * i : 8 * i + 8, :]
        x_s[i, 8:16, :] = tail_sum[8 * i : 8 * i + 8, :]

    def x_copy(i, home):
        to = (n + i) % NARROW
        return pltpu.make_async_remote_copy(
            src_ref=x_s.at[to], dst_ref=x_r.at[home],
            send_sem=x_ss.at[i], recv_sem=x_rs.at[i],
            device_id=(w, to), device_id_type=MESH,
        )

    for i in range(1, NARROW):
        x_copy(i, n).start()
    x_r[n] = x_s[n]
    for i in range(1, NARROW):
        x_copy(i, (n + NARROW - i) % NARROW).wait_recv()
    total = x_r[0] + x_r[1] + x_r[2] + x_r[3]
    coupling = jnp.concatenate([total[0:8, :], total[8:16, :]], axis=1)[:, 0:NC]
    update = (1.0 - DAMPING) * rhs - coupling
    two = one + DAMPING * jacobi(inverse, update)
    fine_o[...] = jnp.dot(two, pt[...], precision=PRECISE, preferred_element_type=jnp.float32)

    def finish(offset, _):
        to, source = partner(offset, 1), partner(offset, -1)
        for copy in (main_copy, rem_copy):
            copy(offset, to, source).wait_recv()
        for copy in (main_copy, rem_copy, y_copy):
            copy(offset, to, w).wait_send()
        return 0

    lax.fori_loop(1, WIDE, finish, 0)

    def finish_spread(q, _):
        g_copy(q, zq).wait_send()
        return 0

    lax.fori_loop(1, 16, finish_spread, 0)
    core_copy(core).wait_send()
    for i in range(1, NARROW):
        x_copy(i, n).wait_send()
        v_copy(i, n).wait_send()
    own_main.wait()
    own_rem.wait()


def exchange(elems, slots, face_blocks, pt, residual, inverse):
    hbm = pl.BlockSpec(memory_space=pltpu.HBM)
    vmem = pl.BlockSpec(memory_space=pltpu.VMEM)
    anywhere = pl.BlockSpec(memory_space=pl.ANY)
    f32, bf16, dma = jnp.float32, jnp.bfloat16, pltpu.SemaphoreType.DMA
    return pl.pallas_call(
        exchange_kernel,
        out_shape=[
            jax.ShapeDtypeStruct((8, NF), f32),
            jax.ShapeDtypeStruct((SLOTS, ROWS, 128), f32),
            jax.ShapeDtypeStruct((SLOTS, 8, 128), f32),
        ],
        in_specs=[hbm] * 6,
        out_specs=[vmem, anywhere, anywhere],
        scratch_shapes=[
            pltpu.SMEM((2, FACES), jnp.int32),
            pltpu.SMEM((WIDE * OWN,), jnp.int32),
            pltpu.VMEM((8, 128), jnp.int32),
            pltpu.SMEM((8, 128), jnp.int32),
            pltpu.VMEM((NC, NF), f32),
            pltpu.VMEM((8, NF), f32),
            pltpu.VMEM((NC, 8, NC), f32),
            pltpu.VMEM((FACES, NF, NF), f32),
            pltpu.VMEM((256, NF), f32),
            pltpu.VMEM((NF, 256), bf16),
            pltpu.VMEM((NF, 256), bf16),
            pltpu.VMEM((144, NF), bf16),
            pltpu.VMEM((144, NF), bf16),
            pltpu.VMEM((SLOTS, ROWS, 128), f32),
            pltpu.VMEM((SLOTS, 8, 128), f32),
            pltpu.VMEM((SLOTS, ROWS, 128), f32),
            pltpu.VMEM((ROWS, 128), f32),
            pltpu.VMEM((WIDE, 8, 128), f32),
            pltpu.VMEM((WIDE, 8, 128), f32),
            pltpu.VMEM((NARROW, 16, 128), f32),
            pltpu.VMEM((NARROW, 16, 128), f32),
            pltpu.VMEM((NARROW, WIDE, 2, 8, 128), f32),
            dma((5,)),
            dma(()),
            dma((5,)),
        ]
        + [dma((WIDE,))] * 6
        + [dma((16,))] * 2
        + [dma((NARROW,))] * 4
        + [dma((2,))] * 2,
        compiler_params=pltpu.CompilerParams(
            collective_id=0, has_side_effects=True, vmem_limit_bytes=42 << 20
        ),
        cost_estimate=pl.CostEstimate(flops=10**10, bytes_accessed=35 * 10**6, transcendentals=0),
        name="exchange",
    )(elems, slots, face_blocks, pt, residual, inverse)


def unpack_kernel(main, rem, fine_in, out, fine, edge):
    i = pl.program_id(0)
    rest = NC - 128

    def row(a):
        return main[pl.ds(a, SLOTS, stride=ROWS), :].T

    @pl.when(i == 0)
    def _():
        fine[...] = fine_in[...]
        for c in range(rest):
            edge[c] = rem[pl.ds(c, SLOTS, stride=8), :].T

    for j in range(NC // PART):

        @pl.when(i == j)
        def _(j=j):
            for r in range(PART):
                out[r, 0:128, :] = row(j * PART + r)
            size = min(PART, 128 - j * PART)
            for c in range(rest):
                out[0:size, 128 + c, :] = edge[c, j * PART : j * PART + size, :]
            if size < PART:
                corner = row(NC)
                for r in range(rest):
                    out[size + r, 128:NC, :] = corner[8 * r : 8 * r + rest, :]


def unpack(main, rem, fine):
    vmem = pl.BlockSpec(memory_space=pltpu.VMEM)
    return pl.pallas_call(
        unpack_kernel,
        grid=(NC // PART,),
        out_shape=[
            jax.ShapeDtypeStruct((NC, NC, SLOTS), jnp.float32),
            jax.ShapeDtypeStruct((8, NF), jnp.float32),
        ],
        in_specs=[vmem] * 3,
        out_specs=[
            pl.BlockSpec((PART, NC, SLOTS), lambda i: (i, 0, 0)),
            pl.BlockSpec((8, NF), lambda i: (0, 0)),
        ],
        scratch_shapes=[pltpu.VMEM((NC - 128, 128, SLOTS), jnp.float32)],
        compiler_params=pltpu.CompilerParams(vmem_limit_bytes=40 << 20),
        name="unpack",
    )(main, rem, fine)


def local(face_blocks, face_elems, coarse_slot, prolong, fine_residual, block_inverse):
    inputs = (
        face_elems.T, coarse_slot, face_blocks, prolong.T, fine_residual, jnp.transpose(block_inverse, (1, 0, 2))
    )
    fine, main, rem = exchange(*(pltpu.with_memory_space_constraint(x, pltpu.HBM) for x in inputs))
    owned, fine = unpack(main.reshape(SLOTS * ROWS, 128), rem.reshape(SLOTS * 8, 128), fine)
    return fine, jnp.transpose(owned, (2, 0, 1))


def solution(mesh):
    placed = (
        P(("wide", "narrow"), None, None),
        P(("wide", "narrow"), None),
        P(),
        P(),
        P(("wide", "narrow"), None),
        P(("wide", "narrow"), None, None),
    )
    return jax.shard_map(
        local,
        mesh=mesh,
        in_specs=placed,
        out_specs=(P(("wide", "narrow"), None), P(("wide", "narrow"), None, None)),
        check_vma=False,
    )
```

```python
import functools

import jax
import jax.numpy as jnp
from jax import lax
from jax.experimental import pallas as pl
from jax.experimental.pallas import tpu as pltpu
from jax.sharding import PartitionSpec as P

DAMPING = 0.7
PRECISE = lax.Precision.HIGHEST
MESH = pl.DeviceIdType.MESH

NF = 320
NC = 135
ROWS = 136
PART = 45
FACES = 40
WIDE = 32
NARROW = 4
CAP = 3
SLOTS = WIDE * CAP
OWN = 32
PAIRS = (
    (1, 1), (3, 3), (1, 3), (3, 1), (2, 1), (0, 3), (2, 3), (0, 1),
    (1, 2), (3, 0), (3, 2), (1, 0), (2, 0), (0, 2), (2, 2),
)
CODES = tuple(
    sum((4 * dz + dy) * 16**i for i, (dz, dy) in enumerate(PAIRS[at : at + 7])) for at in (0, 7, 14)
)
CORE_AT, NARROW_AT = 2, 5
HELD = 26


def offset_at(step):
    last, near = step // 28, step // 30
    pair = (step // 4 * 2 + step % 2) * (1 - last) + 14 * last
    core = step // 2 % 2 * (1 - last) + (step - 28) * last
    part = pair // 7
    first, second, third = (part - 1) * (part - 2) // 2, part * (2 - part), part * (part - 1) // 2
    code = CODES[0] * first + CODES[1] * second + CODES[2] * third
    offset = lax.shift_right_logical(code, 4 * (pair % 7)) % 16 * 2 + core
    return offset * (1 - near) + (31 - step) * near


def slot_words(faces, slots):
    lane = lax.broadcasted_iota(jnp.int32, (1, 128), 1)

    def place(f, words):
        first, second, third = words
        row = slots[faces[0, f]]
        word = (1 << 21) + (row & (OWN - 1)) * 65536 + slots[faces[1, f]] * 64 + f
        here = lane == lax.shift_right_logical(row, 5)
        third = jnp.where(here & (second > 0), word, third)
        second = jnp.where(here & (first > 0) & (second == 0), word, second)
        first = jnp.where(here & (first == 0), word, first)
        return first, second, third

    empty = jnp.zeros((1, 128), jnp.int32)
    return lax.fori_loop(0, FACES, place, (empty, empty, empty), unroll=4)


def shifted(word, by, bits):
    return lax.shift_right_logical(word, by) & ((1 << bits) - 1)


def split(x):
    high = x.astype(jnp.bfloat16)
    return high, (x - high.astype(jnp.float32)).astype(jnp.bfloat16)


def dot(a, b):
    return jnp.dot(a, b, preferred_element_type=jnp.float32)


def dot_t(a, b):
    return lax.dot_general(
        a, b, (((1,), (1,)), ((), ())), precision=PRECISE, preferred_element_type=jnp.float32
    )


def jacobi(inverse, vectors):
    row = lax.broadcasted_iota(jnp.int32, (8, NC), 0)
    out = jnp.zeros((8, NC), jnp.float32)
    for s in range(8):
        out = jnp.where(row == s, dot_t(vectors, inverse[:, s, :]), out)
    return out


def exchange_kernel(
    elems_hbm, slots_hbm, faces_hbm, pt_hbm, residual_hbm, inverse_hbm,
    fine_o, main_o, rem_o,
    elems, slots, words, word, pt, residual, inverse, faces, wide_pt, p_hi, p_lo, pt_hi, pt_lo, main_s, rem_s, edge_s, sums, y_s, y_r, x_s, x_r,
    values,
    in_sem, word_sem, face_sem, main_ss, main_rs, rem_ss, rem_rs, y_ss, y_rs, g_ss, g_rs, x_ss, x_rs, v_ss, v_rs,
    core_sem, own_sem,
):
    w = lax.axis_index("wide")
    n = lax.axis_index("narrow")

    def load(i):
        part = pl.ds(i * 5, 5)
        return pltpu.make_async_copy(faces_hbm.at[part], faces.at[part], face_sem.at[i])

    inputs = [
        pltpu.make_async_copy(source, target, in_sem.at[i])
        for i, (source, target) in enumerate(
            ((elems_hbm, elems), (slots_hbm, slots), (pt_hbm, pt), (residual_hbm, residual), (inverse_hbm, inverse))
        )
    ]
    for copy in inputs:
        copy.start()
    for i in range(8):
        load(i).start()

    def partner(offset, sign):
        z, y, c = w // 8, (w // 2) % 4, w % 2
        dz, dy, dc = offset // 8, (offset // 2) % 4, offset % 2
        return ((z + sign * dz + 4) % 4) * 8 + ((y + sign * dy + 4) % 4) * 2 + (c + dc) % 2

    barrier = pltpu.get_barrier_semaphore()

    def greet(i, _):
        pl.semaphore_signal(barrier, inc=1, device_id=(partner(i, 1), n), device_id_type=MESH)
        return 0

    lax.fori_loop(1, WIDE, greet, 0)
    for i in range(1, NARROW):
        pl.semaphore_signal(barrier, inc=1, device_id=(w, (n + i) % NARROW), device_id_type=MESH)

    for copy in inputs[0:2]:
        copy.wait()
    words[...] = jnp.zeros_like(words)
    for i, row in enumerate(slot_words(elems, slots)):
        words[i : i + 1, :] = row
    fetch = pltpu.make_async_copy(words, word, word_sem)
    fetch.start()
    for copy in inputs[2:5]:
        copy.wait()
    wide_pt[...] = jnp.zeros_like(wide_pt)
    wide_pt[0:NC, :] = pt[...]
    pt_hi[...], pt_lo[...] = split(wide_pt[0:144, :])
    p_hi[...], p_lo[...] = split(wide_pt[...].T)

    rhs = dot_t(residual[...], pt[...])
    one = DAMPING * jacobi(inverse, rhs)
    zq, core = w // 2, w % 2
    values[n, core * 16 + zq, 0] = one[:, 0:128]
    values[n, core * 16 + zq, 1] = jnp.pad(one[:, 128:NC], ((0, 0), (0, 256 - NC)))

    def v_copy(i, home):
        return pltpu.make_async_remote_copy(
            src_ref=values.at[n], dst_ref=values.at[home], send_sem=v_ss.at[i], recv_sem=v_rs.at[i],
            device_id=(w, (n + i) % NARROW), device_id_type=MESH,
        )

    def g_copy(q, home):
        chip = (zq // 4 + q // 4) % 4 * 4 + (zq % 4 + q % 4) % 4
        return pltpu.make_async_remote_copy(
            src_ref=values.at[n, core * 16 + zq], dst_ref=values.at[n, core * 16 + home],
            send_sem=g_ss.at[q], recv_sem=g_rs.at[q],
            device_id=(chip * 2 + core, n), device_id_type=MESH,
        )

    def core_copy(half):
        part = pl.ds(half * 16, 16)
        return pltpu.make_async_remote_copy(
            src_ref=values.at[n, part], dst_ref=values.at[n, part],
            send_sem=core_sem.at[0], recv_sem=core_sem.at[1],
            device_id=(zq * 2 + 1 - core, n), device_id_type=MESH,
        )

    lane = lax.broadcasted_iota(jnp.int32, (ROWS, 128), 1)
    sub = lax.broadcasted_iota(jnp.int32, (ROWS, 1), 0)
    sums[...] = jnp.where(lax.broadcasted_iota(jnp.int32, (ROWS, 128), 0) == NC, -1.0, 0.0)

    def main_copy(offset, to, home):
        return pltpu.make_async_remote_copy(
            src_ref=main_s.at[pl.ds(to * CAP, CAP)],
            dst_ref=main_o.at[pl.ds(home * CAP, CAP)],
            send_sem=main_ss.at[offset], recv_sem=main_rs.at[offset],
            device_id=(to, n), device_id_type=MESH,
        )

    def rem_copy(offset, to, home):
        return pltpu.make_async_remote_copy(
            src_ref=rem_s.at[pl.ds(to * CAP, CAP)],
            dst_ref=rem_o.at[pl.ds(home * CAP, CAP)],
            send_sem=rem_ss.at[offset], recv_sem=rem_rs.at[offset],
            device_id=(to, n), device_id_type=MESH,
        )

    def y_copy(offset, to, home):
        return pltpu.make_async_remote_copy(
            src_ref=y_s.at[to], dst_ref=y_r.at[home],
            send_sem=y_ss.at[offset], recv_sem=y_rs.at[offset],
            device_id=(to, n), device_id_type=MESH,
        )

    def compute(to):
        applied = []
        for k in range(CAP):
            high, low = split(faces[shifted(word[k, to], 0, 6)])
            applied.append(dot(high, p_hi[...]) + dot(low, p_hi[...]) + dot(high, p_lo[...]))
        for k in range(CAP):
            s = to * CAP + k
            high, low = split(applied[k])
            both = dot(pt_hi[...], high) + dot(pt_lo[...], high) + dot(pt_hi[...], low)
            both = jnp.where(shifted(word[k, to], 21, 1) > 0, both[0:ROWS, :], 0.0)
            edge = both[:, 128:256]
            main_s[s] = both[:, 0:128]
            corner = pltpu.roll(edge[128:ROWS, :], 0, 1, stride=8, stride_axis=0)
            main_s[s, NC:ROWS, :] = jnp.sum(corner, axis=0, keepdims=True)
            rem_s[s] = edge[0:128, :].T[0:8, :]
            edge_s[s] = edge

    pl.semaphore_wait(barrier, WIDE + NARROW - 2)

    def spread(q, _):
        g_copy(q, zq).start()
        return 0

    lax.fori_loop(1, 16, spread, 0)
    for i in range(8):
        load(i).wait()
    fetch.wait()

    def send(step, _):
        offset = offset_at(step)
        to = partner(offset, 1)
        compute(to)

        @pl.when((step < HELD) | (step == WIDE - 2))
        def _():
            main_copy(offset, to, w).start()
            rem_copy(offset, to, w).start()

        @pl.when(step == CORE_AT)
        def _():
            def arrive(q, _):
                home = (zq // 4 - q // 4 + 4) % 4 * 4 + (zq % 4 - q % 4 + 4) % 4
                g_copy(q, home).wait_recv()
                return 0

            lax.fori_loop(1, 16, arrive, 0)
            core_copy(core).start()

        @pl.when(step == NARROW_AT)
        def _():
            core_copy(1 - core).wait_recv()
            for i in range(1, NARROW):
                v_copy(i, n).start()

        return 0

    lax.fori_loop(0, WIDE, send, 0)
    mine = pl.ds(w * CAP, CAP)
    own_main = pltpu.make_async_copy(main_s.at[mine], main_o.at[mine], own_sem.at[0])
    own_rem = pltpu.make_async_copy(rem_s.at[mine], rem_o.at[mine], own_sem.at[1])
    own_main.start()
    own_rem.start()
    for i in range(1, NARROW):
        v_copy(i, (n + NARROW - i) % NARROW).wait_recv()

    def apply(to, _):
        for k in range(CAP):
            s = to * CAP + k
            row = pl.ds(shifted(word[k, to], 6, 3), 1)
            narrow = shifted(word[k, to], 9, 2)
            at = shifted(word[k, to], 11, 1) * 16 + shifted(word[k, to], 12, 4)
            head, tail = values[narrow, at, 0, row, :], values[narrow, at, 1, row, :]
            y = jnp.sum(main_s[s] * head + edge_s[s] * tail, axis=1, keepdims=True)
            label = shifted(word[k, to], 16, 5) * shifted(word[k, to], 21, 1) - 1 + shifted(word[k, to], 21, 1)
            y = jnp.where(sub == NC, label.astype(jnp.float32), y)
            sums[...] = jnp.where(lane == to * 4 + k, y, sums[...])
        return 0

    lax.fori_loop(0, WIDE, apply, 0)

    by_slot = jnp.concatenate([sums[0:128, :].T, jnp.pad(sums[128:ROWS, :].T, ((0, 0), (0, 120)))], axis=0)
    for to in range(WIDE):
        y_s[to, 0:3, :] = by_slot[4 * to : 4 * to + 3, :]
        y_s[to, 3:6, :] = by_slot[128 + 4 * to : 128 + 4 * to + 3, :]
        y_s[to, 6:8, :] = jnp.zeros((2, 128), jnp.float32)

    def send_y(offset, _):
        y_copy(offset, partner(offset, 1), w).start()
        return 0

    lax.fori_loop(1, WIDE, send_y, 0)
    y_r[w] = y_s[w]

    def send_held(step, _):
        offset = offset_at(step)
        to = partner(offset, 1)
        main_copy(offset, to, w).start()
        rem_copy(offset, to, w).start()
        return 0

    lax.fori_loop(HELD, WIDE - 2, send_held, 0)

    def wait_y(offset, _):
        y_copy(offset, partner(offset, 1), partner(offset, -1)).wait_recv()
        return 0

    lax.fori_loop(1, WIDE, wait_y, 0)

    terms = y_r[...].reshape(WIDE * 8, 128)
    labels = terms.T[7:8, :]
    place = lax.broadcasted_iota(jnp.int32, (OWN, WIDE * 8), 1) % 8
    of_row = lax.broadcasted_iota(jnp.int32, (OWN, WIDE * 8), 0).astype(jnp.float32)
    tail = jnp.where((labels == of_row) & (place >= 3) & (place < 6), 1.0, 0.0)
    head = pltpu.roll(tail, WIDE * 8 - 3, 1)
    head_sum = jnp.dot(head, terms, precision=PRECISE, preferred_element_type=jnp.float32)
    tail_sum = jnp.dot(tail, terms, precision=PRECISE, preferred_element_type=jnp.float32)
    for i in range(NARROW):
        x_s[i, 0:8, :] = head_sum[8 * i : 8 * i + 8, :]
        x_s[i, 8:16, :] = tail_sum[8 * i : 8 * i + 8, :]

    def x_copy(i, home):
        to = (n + i) % NARROW
        return pltpu.make_async_remote_copy(
            src_ref=x_s.at[to], dst_ref=x_r.at[home],
            send_sem=x_ss.at[i], recv_sem=x_rs.at[i],
            device_id=(w, to), device_id_type=MESH,
        )

    for i in range(1, NARROW):
        x_copy(i, n).start()
    x_r[n] = x_s[n]
    for i in range(1, NARROW):
        x_copy(i, (n + NARROW - i) % NARROW).wait_recv()
    total = x_r[0] + x_r[1] + x_r[2] + x_r[3]
    coupling = jnp.concatenate([total[0:8, :], total[8:16, :]], axis=1)[:, 0:NC]
    update = (1.0 - DAMPING) * rhs - coupling
    two = one + DAMPING * jacobi(inverse, update)
    fine_o[...] = jnp.dot(two, pt[...], precision=PRECISE, preferred_element_type=jnp.float32)

    def finish(offset, _):
        to, source = partner(offset, 1), partner(offset, -1)
        for copy in (main_copy, rem_copy):
            copy(offset, to, source).wait_recv()
        for copy in (main_copy, rem_copy, y_copy):
            copy(offset, to, w).wait_send()
        return 0

    lax.fori_loop(1, WIDE, finish, 0)

    def finish_spread(q, _):
        g_copy(q, zq).wait_send()
        return 0

    lax.fori_loop(1, 16, finish_spread, 0)
    core_copy(core).wait_send()
    for i in range(1, NARROW):
        x_copy(i, n).wait_send()
        v_copy(i, n).wait_send()
    own_main.wait()
    own_rem.wait()


def exchange(elems, slots, face_blocks, pt, residual, inverse):
    hbm = pl.BlockSpec(memory_space=pltpu.HBM)
    vmem = pl.BlockSpec(memory_space=pltpu.VMEM)
    anywhere = pl.BlockSpec(memory_space=pl.ANY)
    f32, bf16, dma = jnp.float32, jnp.bfloat16, pltpu.SemaphoreType.DMA
    return pl.pallas_call(
        exchange_kernel,
        out_shape=[
            jax.ShapeDtypeStruct((8, NF), f32),
            jax.ShapeDtypeStruct((SLOTS, ROWS, 128), f32),
            jax.ShapeDtypeStruct((SLOTS, 8, 128), f32),
        ],
        in_specs=[hbm] * 6,
        out_specs=[vmem, anywhere, anywhere],
        scratch_shapes=[
            pltpu.SMEM((2, FACES), jnp.int32),
            pltpu.SMEM((WIDE * OWN,), jnp.int32),
            pltpu.VMEM((8, 128), jnp.int32),
            pltpu.SMEM((8, 128), jnp.int32),
            pltpu.VMEM((NC, NF), f32),
            pltpu.VMEM((8, NF), f32),
            pltpu.VMEM((NC, 8, NC), f32),
            pltpu.VMEM((FACES, NF, NF), f32),
            pltpu.VMEM((256, NF), f32),
            pltpu.VMEM((NF, 256), bf16),
            pltpu.VMEM((NF, 256), bf16),
            pltpu.VMEM((144, NF), bf16),
            pltpu.VMEM((144, NF), bf16),
            pltpu.VMEM((SLOTS, ROWS, 128), f32),
            pltpu.VMEM((SLOTS, 8, 128), f32),
            pltpu.VMEM((SLOTS, ROWS, 128), f32),
            pltpu.VMEM((ROWS, 128), f32),
            pltpu.VMEM((WIDE, 8, 128), f32),
            pltpu.VMEM((WIDE, 8, 128), f32),
            pltpu.VMEM((NARROW, 16, 128), f32),
            pltpu.VMEM((NARROW, 16, 128), f32),
            pltpu.VMEM((NARROW, WIDE, 2, 8, 128), f32),
            dma((5,)),
            dma(()),
            dma((8,)),
        ]
        + [dma((WIDE,))] * 6
        + [dma((16,))] * 2
        + [dma((NARROW,))] * 4
        + [dma((2,))] * 2,
        compiler_params=pltpu.CompilerParams(
            collective_id=0, has_side_effects=True, vmem_limit_bytes=42 << 20
        ),
        cost_estimate=pl.CostEstimate(flops=10**10, bytes_accessed=35 * 10**6, transcendentals=0),
        name="exchange",
    )(elems, slots, face_blocks, pt, residual, inverse)


def unpack_kernel(main, rem, fine_in, out, fine, edge):
    i = pl.program_id(0)
    rest = NC - 128

    def row(a):
        return main[pl.ds(a, SLOTS, stride=ROWS), :].T

    @pl.when(i == 0)
    def _():
        fine[...] = fine_in[...]
        for c in range(rest):
            edge[c] = rem[pl.ds(c, SLOTS, stride=8), :].T

    for j in range(NC // PART):

        @pl.when(i == j)
        def _(j=j):
            for r in range(PART):
                out[r, 0:128, :] = row(j * PART + r)
            size = min(PART, 128 - j * PART)
            for c in range(rest):
                out[0:size, 128 + c, :] = edge[c, j * PART : j * PART + size, :]
            if size < PART:
                corner = row(NC)
                for r in range(rest):
                    out[size + r, 128:NC, :] = corner[8 * r : 8 * r + rest, :]


def unpack(main, rem, fine):
    vmem = pl.BlockSpec(memory_space=pltpu.VMEM)
    return pl.pallas_call(
        unpack_kernel,
        grid=(NC // PART,),
        out_shape=[
            jax.ShapeDtypeStruct((NC, NC, SLOTS), jnp.float32),
            jax.ShapeDtypeStruct((8, NF), jnp.float32),
        ],
        in_specs=[vmem] * 3,
        out_specs=[
            pl.BlockSpec((PART, NC, SLOTS), lambda i: (i, 0, 0)),
            pl.BlockSpec((8, NF), lambda i: (0, 0)),
        ],
        scratch_shapes=[pltpu.VMEM((NC - 128, 128, SLOTS), jnp.float32)],
        compiler_params=pltpu.CompilerParams(vmem_limit_bytes=40 << 20),
        name="unpack",
    )(main, rem, fine)


def local(face_blocks, face_elems, coarse_slot, prolong, fine_residual, block_inverse):
    inputs = (
        face_elems.T, coarse_slot, face_blocks, prolong.T, fine_residual, jnp.transpose(block_inverse, (1, 0, 2))
    )
    fine, main, rem = exchange(*(pltpu.with_memory_space_constraint(x, pltpu.HBM) for x in inputs))
    owned, fine = unpack(main.reshape(SLOTS * ROWS, 128), rem.reshape(SLOTS * 8, 128), fine)
    return fine, jnp.transpose(owned, (2, 0, 1))


def solution(mesh):
    placed = (
        P(("wide", "narrow"), None, None),
        P(("wide", "narrow"), None),
        P(),
        P(),
        P(("wide", "narrow"), None),
        P(("wide", "narrow"), None, None),
    )
    return jax.shard_map(
        local,
        mesh=mesh,
        in_specs=placed,
        out_specs=(P(("wide", "narrow"), None), P(("wide", "narrow"), None, None)),
        check_vma=False,
    )
```
